32 devices in a mesh: samp: 16 (over z, y, x), mark: 2 (over core).
Axes of the slice: x: 2, y: 2, z: 4, core: 2. Of those that a mesh axis runs over, the one named last changes fastest.
Arguments:
- dosage: bfloat16 [8192, 512], P('samp', 'mark'), may hold values from 0 to 2
- alt_count: int32 [512], P('mark'), may hold values from 40000 to 759999
- obs_count: int32 [512], P('mark'), may hold values from 400000 to 500000
- sample_weight: float32 [8192], P('samp'), may hold values from 0.25 to 12, as said below
- test_matrix: bfloat16 [512, 256], P(('mark', 'samp')), may hold values from -6 to 6
Outputs:
- basis: float32 [8192, 256], P(('samp', 'mark'))
- loadings: float32 [512, 256], P(('mark', 'samp'))
The draws below stay inside these ranges and needn't reach their ends.
Inputs may be any that keep to these rules, and one draw needn't show every extreme that they name: `sample_weight`: every weight is positive.
All inputs are finite; a program needn't handle non-finite values.
Results may differ from the reference program's by a relative error of at most 0.004.
Values may be sent and summed in bfloat16 or wider, within the bound.
No kernel may reach another device: no remote copies, remote signals or barrier semaphores. Data moves between devices by JAX's collectives and lax.ppermute only.
A program may use at most 64 MiB of HBM per device.

```python
import math
import jax
import jax.numpy as jnp
from jax import lax

K = 256
RS = 512
NS = 8192
NM = 512
N_SAMP = 16


def draw_sample_weight(key, part):
    position = jnp.arange(NS, dtype=jnp.float32)
    rising = 1.0 + 2.0 * position / (NS - 1)
    jitter = jnp.exp(jax.random.uniform(key, (NS,), jnp.float32, -math.log(4.0), math.log(4.0)))
    return rising * jitter


def with_ends(values, own_key, low, high):
    longest = values.shape.index(max(values.shape))
    spots = []
    for shift in (0, 1):
        where = [jax.random.randint(jax.random.fold_in(own_key, axis), (), 0, length) for axis, length in enumerate(values.shape)]
        where[longest] = (where[longest] + shift) % values.shape[longest]
        spots.append(tuple(where))
    return values.at[spots[0]].set(low).at[spots[1]].set(high)


def levels(stream_key, dims, split, smallest, high):
    def one(axis_at, shards_of):
        heights = jax.random.uniform(jax.random.fold_in(jax.random.fold_in(stream_key, 6), axis_at), (shards_of,), jnp.float32, smallest / len(split), high / len(split))
        return jnp.repeat(jnp.exp(heights), dims[axis_at] // shards_of).reshape((-1,) + (1,) * (len(dims) - axis_at - 1))

    level = one(*split[0])
    for cut in split[1:]:
        level = level * one(*cut)
    return level


def scatter_about(own_key, dims, deviation, most, split=(), kind=jnp.bfloat16):
    gain = levels(own_key, dims, split, -0.22, 0.18) if split else 1.0
    entries = jax.random.normal(own_key, dims, jnp.float32) * deviation * gain
    return jnp.minimum(jnp.maximum(entries, -most), most).astype(kind)


def setup_inputs(seed: int = 0) -> dict:
    key_of = jax.random.split(jax.random.key(seed), 6)
    dosage = jnp.clip(2.0 * jax.random.uniform(key_of[0], (NS, NM), jnp.float32) ** levels(key_of[0], (NS, NM), ((0, 16), (1, 2)), -0.2, 0.2), 0.0, 2.0).astype(jnp.bfloat16)
    alt_count = with_ends(jax.random.randint(key_of[1], (NM,), 40000, 760000), jax.random.fold_in(key_of[1], 1), 40000, 759999).astype(jnp.int32)
    obs_count = with_ends(jax.random.randint(key_of[2], (NM,), 400000, 500001), jax.random.fold_in(key_of[2], 1), 400000, 500000).astype(jnp.int32)
    sample_weight = draw_sample_weight(jax.random.fold_in(key_of[5], 71), 0)
    test_matrix = scatter_about(key_of[4], (NM, K), 1.0, 6.0, ((0, 32),))
    return dict(dosage=dosage, alt_count=alt_count, obs_count=obs_count, sample_weight=sample_weight, test_matrix=test_matrix)


def standardize(block, weights, freq, scale):
    return (jnp.sqrt(weights)[:, None] * (block.astype(jnp.float32) - 2.0 * freq) * scale).astype(jnp.bfloat16)

def reference(dosage, alt_count, obs_count, sample_weight, test_matrix):
    freq = alt_count.astype(jnp.float32) / (2.0 * obs_count.astype(jnp.float32))
    scale = 1.0 / jnp.sqrt(2.0 * freq * (1.0 - freq))
    blocks = dosage.reshape(N_SAMP, RS, NM)
    weight_blocks = sample_weight.reshape(N_SAMP, RS)

    def sketch_block(pair):
        standard = standardize(pair[0], pair[1], freq, scale)
        return jnp.dot(standard.astype(jnp.float32), test_matrix.astype(jnp.float32), preferred_element_type=jnp.float32)
    sketch = lax.map(sketch_block, (blocks, weight_blocks)).reshape(NS, K)
    gram = lax.dot_general(sketch.astype(jnp.float32), sketch.astype(jnp.float32), (((0,), (0,)), ((), ())), precision=lax.Precision.HIGHEST, preferred_element_type=jnp.float32)
    lower = jnp.linalg.cholesky(gram)
    basis = math.sqrt(NS) * lax.linalg.triangular_solve(lower, sketch, left_side=False, lower=True, transpose_a=True)
    sketch_round = sketch.astype(jnp.bfloat16).reshape(N_SAMP, RS, K)

    def project_block(total, triple):
        standard = standardize(triple[0], triple[1], freq, scale)
        term = lax.dot_general(standard.astype(jnp.float32), triple[2].astype(jnp.float32), (((0,), (0,)), ((), ())), preferred_element_type=jnp.float32)
        return (total + term, None)
    projected, unused = lax.scan(project_block, jnp.zeros((NM, K), jnp.float32), (blocks, weight_blocks, sketch_round))
    loadings = lax.linalg.triangular_solve(lower, projected, left_side=False, lower=True, transpose_a=True)
    return (basis, loadings)
```

```python
import math

import jax
import jax.numpy as jnp
from jax import lax
from jax.experimental import pallas as pl
from jax.experimental.pallas import tpu as pltpu
from jax.sharding import PartitionSpec as P

F32, BF16 = jnp.float32, jnp.bfloat16
HALF = 128
BLOCK = 64
PIVOTS = 8
VMEM = pltpu.VMEM


def dot(a, b, ca, cb, precision=lax.Precision.HIGHEST):
    return lax.dot_general(
        a, b, (((ca,), (cb,)), ((), ())), precision=precision, preferred_element_type=F32
    )


def pieces(x):
    high = x.astype(BF16)
    rest = x - high.astype(F32)
    mid = rest.astype(BF16)
    return high, mid, (rest - mid.astype(F32)).astype(BF16)


def dot_pieces(parts, b, ca, cb):
    terms = [dot(p, b, ca, cb, lax.Precision.DEFAULT) for p in parts]
    return terms[0] + (terms[1] + terms[2])


def dot_pieces_right(a, parts, ca, cb):
    terms = [dot(a, p, ca, cb, lax.Precision.DEFAULT) for p in parts]
    return terms[0] + (terms[1] + terms[2])


def standard_kernel(dosage, alt, obs, weight, out):
    freq = alt[...].astype(F32) / (2.0 * obs[...].astype(F32))
    scale = 1.0 / jnp.sqrt(2.0 * freq * (1.0 - freq))
    root = jnp.sqrt(weight[...])
    rows, cols = dosage.shape
    for r in range(0, rows, HALF):
        column = jnp.transpose(jnp.broadcast_to(root[:, r : r + HALF], (HALF, HALF)))
        for c in range(0, cols, HALF):
            x = dosage[r : r + HALF, c : c + HALF].astype(F32)
            f = freq[:, c : c + HALF]
            out[r : r + HALF, c : c + HALF] = (column * (x - 2.0 * f) * scale[:, c : c + HALF]).astype(BF16)


def moment_kernel(place, own, other, out):
    core = place[1]
    low, high = own[:, :HALF], own[:, HALF:]
    first = other[:, pl.ds(pl.multiple_of(core * HALF, HALF), HALF)]
    second = other[:, pl.ds(pl.multiple_of((1 - core) * HALF, HALF), HALF)]
    for i, (a, b) in enumerate(((low, low), (high, low), (high, high), (low, first), (high, second))):
        out[i * HALF : (i + 1) * HALF, :] = dot(a, b, 0, 0, lax.Precision.DEFAULT)


def eliminate(groups, width):
    shape = (8, width)
    lane = lax.broadcasted_iota(jnp.int32, shape, 1)
    sub = lax.broadcasted_iota(jnp.int32, shape, 0)
    groups, result = list(groups), []
    for g in range(len(groups)):
        j = 8 * g
        rows = [jnp.broadcast_to(groups[g][k : k + 1, :], shape) for k in range(8)]
        a = {
            (i, k): jnp.broadcast_to(groups[g][i : i + 1, j + k : j + k + 1], shape)
            for i in range(8)
            for k in range(i + 1)
        }
        inside = (lane >= j) & (lane < j + 8)
        root, done, low = [], [], {}
        block = jnp.zeros(shape, F32)
        for k in range(8):
            q = lax.rsqrt(a[k, k])
            root.append(q)
            for i in range(k + 1, 8):
                low[i, k] = a[i, k] * q
            for i in range(k + 1, 8):
                for m in range(k + 1, i + 1):
                    a[i, m] = a[i, m] - low[i, k] * low[m, k]
            row = jnp.where(inside, jnp.where(lane == j + k, 1.0, 0.0), rows[k])
            for m in range(k):
                row = row - low[k, m] * done[m]
            done.append(row * q)
            block = jnp.where((sub == k) & (lane <= j + k), done[k], block)
        result.append(block)
        if g + 1 == len(groups):
            break
        update = [None] * 8
        for k in reversed(range(8)):
            x = done[k]
            for m in range(k + 1, 8):
                x = x - low[m, k] * update[m]
            update[k] = x * root[k]
        for n in range(g + 1, len(groups)):
            x = jnp.where(inside, 0.0, groups[n])
            for k in range(8):
                x = x - jnp.broadcast_to(groups[n][:, j + k : j + k + 1], shape) * update[k]
            groups[n] = x
    return result


def inverse_factor(gram, out):
    n = gram.shape[0]
    rest = gram
    for at in range(0, n, BLOCK):
        end = at + BLOCK
        row = rest[:BLOCK]
        inv = jnp.concatenate(eliminate([row[i : i + 8, at:end] for i in range(0, BLOCK, 8)], BLOCK), 0)
        if end < n:
            full = dot(inv, row, 1, 0)
            joined = jnp.concatenate(([full[:, :at]] if at else []) + [inv, full[:, end:]], 1)
            lane = lax.broadcasted_iota(jnp.int32, (BLOCK, n), 1)
            out[at:end, :] = jnp.where(lane < end, joined, 0.0)
            below = rest[BLOCK:]
            lane = lax.broadcasted_iota(jnp.int32, below.shape, 1)
            rest = jnp.where((lane >= at) & (lane < end), 0.0, below) - dot(joined[:, end:], joined, 0, 0)
        else:
            out[at:end, :] = jnp.concatenate([dot(inv, row[:, :at], 1, 0), inv], 1) if at else inv


def final_kernel(
    total, place, blocks, others, test, test_other, standard, standard_other, basis, loadings, moments, inverse, product
):
    samp, core = place[0], place[1]
    side = 2 * HALF
    block = lambda ref, i: ref[i * HALF : (i + 1) * HALF, :]
    for ref, at in ((blocks, 0), (others, side)):
        corner = block(ref, 1)
        moments[at : at + HALF, at : at + HALF] = block(ref, 0)
        moments[at + HALF : at + side, at : at + HALF] = corner
        moments[at : at + HALF, at + HALF : at + side] = corner.T
        moments[at + HALF : at + side, at + HALF : at + side] = block(ref, 2)
    mine, theirs = (block(blocks, 3), block(blocks, 4)), (block(others, 3), block(others, 4))
    for h in range(2):
        column = pl.ds(pl.multiple_of(side + (h + core - 2 * h * core) * HALF, HALF), HALF)
        moments[h * HALF : (h + 1) * HALF, column] = mine[h]
        moments[column, h * HALF : (h + 1) * HALF] = mine[h].T
        away = 1 - core
        column = pl.ds(pl.multiple_of((h + away - 2 * h * away) * HALF, HALF), HALF)
        moments[side + h * HALF : side + (h + 1) * HALF, column] = theirs[h]
        moments[column, side + h * HALF : side + (h + 1) * HALF] = theirs[h].T
    tests = jnp.concatenate([test[...], test_other[...]], 0)
    product[...] = dot_pieces(pieces(moments[...]), tests, 1, 0)
    gram = dot_pieces_right(tests, pieces(product[...]), 0, 0)
    inverse_factor(gram, inverse)
    share = basis.shape[0]
    rows = pl.ds(pl.multiple_of(core * share, share), share)
    sketch = dot(standard[rows, :], test[...], 1, 0, lax.Precision.DEFAULT) + dot(
        standard_other[rows, :], test_other[...], 1, 0, lax.Precision.DEFAULT
    )
    basis[...] = math.sqrt(total) * dot(sketch, inverse[...], 1, 1)
    few = loadings.shape[0]
    own = product[pl.ds(pl.multiple_of(samp * few, few), few), :]
    loadings[...] = dot(own, inverse[...], 1, 1)


def call(kernel, shapes, inputs, place=None, scratch=()):
    vmem = pl.BlockSpec(memory_space=VMEM)
    specs = [vmem] * len(inputs)
    if place is not None:
        specs, inputs = [pl.BlockSpec(memory_space=pltpu.SMEM)] + specs, [place] + list(inputs)
    many = isinstance(shapes, (list, tuple))
    return pl.pallas_call(
        kernel,
        out_shape=shapes,
        in_specs=specs,
        out_specs=[vmem] * len(shapes) if many else vmem,
        scratch_shapes=list(scratch),
        compiler_params=pltpu.CompilerParams(vmem_limit_bytes=24 * 2**20),
    )(*inputs)


def swap(x, axis, bit):
    return lax.ppermute(x, axis, [(i, i ^ bit) for i in range(lax.axis_size(axis))])


def upper(axis, bit):
    return (lax.axis_index(axis) // bit) % 2


def keep_half(x, axis, bit):
    half, up = x.shape[0] // 2, upper(axis, bit)
    kept = lax.dynamic_slice_in_dim(x, up * half, half, 0)
    sent = lax.dynamic_slice_in_dim(x, (1 - up) * half, half, 0)
    return kept + swap(sent, axis, bit)


def join(x, axis, bit):
    got = swap(x, axis, bit)
    return jnp.where(upper(axis, bit) == 0, jnp.concatenate([x, got], 0), jnp.concatenate([got, x], 0))


def sum_over(x, axis):
    bits = [1 << i for i in range((lax.axis_size(axis) - 1).bit_length())]
    half = x.shape[0] // 2
    plans = ((bits[0], bits[2:3] + bits[1:2] + bits[3:]), (bits[1], bits[0:1] + bits[2:]))
    parts = []
    for part, (first, rest) in zip((x[:half], x[half:]), plans):
        part = keep_half(part, axis, first)
        for bit in rest:
            part = part + swap(part, axis, bit)
        parts.append(join(part, axis, first))
    return jnp.concatenate(parts, 0)


def two_marks(dosage, alt_count, obs_count, sample_weight, test_matrix):
    rows, cols = dosage.shape
    few, rank = test_matrix.shape
    samples = rows * lax.axis_size("samp")
    place = jnp.stack([lax.axis_index("samp"), lax.axis_index("mark")]).astype(jnp.int32)
    standard = call(
        standard_kernel,
        jax.ShapeDtypeStruct((rows, cols), BF16),
        [dosage, alt_count.reshape(1, cols), obs_count.reshape(1, cols), sample_weight.reshape(1, rows)],
    )
    standard_other = swap(standard, "mark", 1)
    blocks = call(
        moment_kernel, jax.ShapeDtypeStruct((5 * HALF, HALF), F32), [standard, standard_other], place
    )
    test = test_matrix
    for i in range((lax.axis_size("samp") - 1).bit_length()):
        test = join(test, "samp", 1 << i)
    test_other = swap(test, "mark", 1)
    blocks = sum_over(blocks, "samp")
    others = swap(blocks, "mark", 1)
    kernel = lambda *refs: final_kernel(samples, *refs)
    basis, loadings = call(
        kernel,
        [jax.ShapeDtypeStruct((rows // 2, rank), F32), jax.ShapeDtypeStruct((few, rank), F32)],
        [blocks, others, test, test_other, standard, standard_other],
        place,
        [VMEM((2 * cols, 2 * cols), F32), VMEM((rank, rank), F32), VMEM((2 * cols, rank), F32)],
    )
    return basis, loadings


def any_marks(dosage, alt_count, obs_count, sample_weight, test_matrix):
    freq = alt_count.astype(F32) / (2.0 * obs_count.astype(F32))
    scale = 1.0 / jnp.sqrt(2.0 * freq * (1.0 - freq))
    standard = (jnp.sqrt(sample_weight)[:, None] * (dosage.astype(F32) - 2.0 * freq) * scale).astype(BF16)
    rank = test_matrix.shape[1]
    partial_value = jnp.dot(
        standard, lax.all_gather(test_matrix, "samp", axis=0, tiled=True), preferred_element_type=F32
    )
    share = standard.shape[0] // lax.axis_size("mark")
    sketch = lax.psum(partial_value, "mark")
    own_rows = lax.dynamic_slice_in_dim(sketch, lax.axis_index("mark") * share, share, 0)
    gram = dot(sketch, sketch, 0, 0)
    lower = jnp.linalg.cholesky(lax.psum(gram, "samp"))
    inverse = lax.linalg.triangular_solve(lower, jnp.eye(rank, dtype=F32), left_side=True, lower=True)
    basis = math.sqrt(standard.shape[0] * lax.axis_size("samp")) * dot(own_rows, inverse, 1, 1)
    projected = lax.psum_scatter(
        dot(standard, sketch.astype(BF16), 0, 0, lax.Precision.DEFAULT), "samp", scatter_dimension=0, tiled=True
    )
    return basis, dot(projected, inverse, 1, 1)


def solution(mesh):
    samp, mark = mesh.shape["samp"], mesh.shape["mark"]

    def per_device(dosage, *rest):
        fits = mark == 2 and samp >= 4 and samp & (samp - 1) == 0 and dosage.shape[1] == 2 * HALF
        return (two_marks if fits else any_marks)(dosage, *rest)

    return jax.shard_map(
        per_device,
        mesh=mesh,
        in_specs=(P("samp", "mark"), P("mark"), P("mark"), P("samp"), P(("mark", "samp"), None)),
        out_specs=(P(("samp", "mark"), None), P(("mark", "samp"), None)),
        check_vma=False,
    )
```

```python
import math

import jax
import jax.numpy as jnp
from jax import lax
from jax.experimental import pallas as pl
from jax.experimental.pallas import tpu as pltpu
from jax.sharding import PartitionSpec as P

F32, BF16 = jnp.float32, jnp.bfloat16
HALF = 128
BLOCK = 64
VMEM = pltpu.VMEM


def dot(a, b, ca, cb, precision=lax.Precision.HIGHEST):
    return lax.dot_general(
        a, b, (((ca,), (cb,)), ((), ())), precision=precision, preferred_element_type=F32
    )


def pieces(x):
    high = x.astype(BF16)
    rest = x - high.astype(F32)
    mid = rest.astype(BF16)
    return high, mid, (rest - mid.astype(F32)).astype(BF16)


def dot_pieces(parts, b, ca, cb):
    terms = [dot(p, b, ca, cb, lax.Precision.DEFAULT) for p in parts]
    return terms[0] + (terms[1] + terms[2])


def dot_pieces_right(a, parts, ca, cb):
    terms = [dot(a, p, ca, cb, lax.Precision.DEFAULT) for p in parts]
    return terms[0] + (terms[1] + terms[2])


def standard_kernel(dosage, alt, obs, weight, out):
    freq = alt[...].astype(F32) / (2.0 * obs[...].astype(F32))
    scale = 1.0 / jnp.sqrt(2.0 * freq * (1.0 - freq))
    root = jnp.sqrt(weight[...])
    rows, cols = dosage.shape
    for r in range(0, rows, HALF):
        column = jnp.transpose(jnp.broadcast_to(root[:, r : r + HALF], (HALF, HALF)))
        for c in range(0, cols, HALF):
            x = dosage[r : r + HALF, c : c + HALF].astype(F32)
            f = freq[:, c : c + HALF]
            out[r : r + HALF, c : c + HALF] = (column * (x - 2.0 * f) * scale[:, c : c + HALF]).astype(BF16)


def moment_kernel(place, own, other, out):
    core = place[1]
    low, high = own[:, :HALF], own[:, HALF:]
    first = other[:, pl.ds(pl.multiple_of(core * HALF, HALF), HALF)]
    second = other[:, pl.ds(pl.multiple_of((1 - core) * HALF, HALF), HALF)]
    for i, (a, b) in enumerate(((low, low), (high, low), (high, high), (low, first), (high, second))):
        out[i * HALF : (i + 1) * HALF, :] = dot(a, b, 0, 0, lax.Precision.DEFAULT)


def eliminate(groups, width):
    shape = (8, width)
    lane = lax.broadcasted_iota(jnp.int32, shape, 1)
    sub = lax.broadcasted_iota(jnp.int32, shape, 0)
    spread = lambda x: jnp.broadcast_to(x, shape)
    groups, result = list(groups), []
    for g in range(len(groups)):
        j = 8 * g
        columns = lambda group: [spread(group[:, j + k : j + k + 1]) for k in range(8)]
        rows = [spread(groups[g][k : k + 1, :]) for k in range(8)]
        a = {(i, k): spread(c[i : i + 1, :]) for k, c in enumerate(columns(groups[g])) for i in range(k, 8)}
        inside = (lane >= j) & (lane < j + 8)
        root, done, low = [], [], {}
        block = jnp.zeros(shape, F32)
        for k in range(8):
            q = lax.rsqrt(a[k, k])
            root.append(q)
            for i in range(k + 1, 8):
                low[i, k] = a[i, k] * q
            for i in range(k + 1, 8):
                for m in range(k + 1, i + 1):
                    a[i, m] = a[i, m] - low[i, k] * low[m, k]
            row = jnp.where(inside, jnp.where(lane == j + k, 1.0, 0.0), rows[k])
            for m in range(k):
                row = row - low[k, m] * done[m]
            done.append(row * q)
            block = jnp.where((sub == k) & (lane <= j + k), done[k], block)
        result.append(block)
        if g + 1 == len(groups):
            break
        factors = []
        for k, c in enumerate(columns(groups[g + 1])):
            for m in range(k):
                c = c - factors[m] * low[k, m]
            factors.append(c * root[k])
        x = jnp.where(inside, 0.0, groups[g + 1])
        for k in range(8):
            x = x - factors[k] * done[k]
        groups[g + 1] = x
        update = [None] * 8
        for k in reversed(range(8)):
            x = done[k]
            for m in range(k + 1, 8):
                x = x - low[m, k] * update[m]
            update[k] = x * root[k]
        for n in range(g + 2, len(groups)):
            x = jnp.where(inside, 0.0, groups[n])
            for k, c in enumerate(columns(groups[n])):
                x = x - c * update[k]
            groups[n] = x
    return result


def inverse_factor(gram, out):
    n = gram.shape[0]
    rest, corner = gram, gram[:BLOCK, :BLOCK]
    for at in range(0, n, BLOCK):
        end = at + BLOCK
        row = rest[:BLOCK]
        inv = jnp.concatenate(eliminate([corner[i : i + 8, :] for i in range(0, BLOCK, 8)], BLOCK), 0)
        if end == n:
            out[at:end, :] = jnp.concatenate([dot(inv, row[:, :at], 1, 0), inv], 1) if at else inv
            break
        ahead = dot(inv, row[:, end : end + BLOCK], 1, 0)
        corner = rest[BLOCK : 2 * BLOCK, end : end + BLOCK] - dot(ahead, ahead, 0, 0)
        full = dot(inv, row, 1, 0)
        joined = jnp.concatenate(([full[:, :at]] if at else []) + [inv, full[:, end:]], 1)
        lane = lax.broadcasted_iota(jnp.int32, (BLOCK, n), 1)
        out[at:end, :] = jnp.where(lane < end, joined, 0.0)
        below = rest[BLOCK:]
        lane = lax.broadcasted_iota(jnp.int32, below.shape, 1)
        rest = jnp.where((lane >= at) & (lane < end), 0.0, below) - dot(joined[:, end:], joined, 0, 0)


def final_kernel(
    total, place, blocks, others, test, test_other, standard, standard_other, basis, loadings, moments, inverse, product, gathered
):
    samp, core = place[0], place[1]
    side = 2 * HALF
    block = lambda ref, i: ref[i * HALF : (i + 1) * HALF, :]
    for ref, at in ((blocks, 0), (others, side)):
        corner = block(ref, 1)
        moments[at : at + HALF, at : at + HALF] = block(ref, 0)
        moments[at + HALF : at + side, at : at + HALF] = corner
        moments[at : at + HALF, at + HALF : at + side] = corner.T
        moments[at + HALF : at + side, at + HALF : at + side] = block(ref, 2)
    mine, theirs = (block(blocks, 3), block(blocks, 4)), (block(others, 3), block(others, 4))
    for h in range(2):
        column = pl.ds(pl.multiple_of(side + (h + core - 2 * h * core) * HALF, HALF), HALF)
        moments[h * HALF : (h + 1) * HALF, column] = mine[h]
        moments[column, h * HALF : (h + 1) * HALF] = mine[h].T
        away = 1 - core
        column = pl.ds(pl.multiple_of((h + away - 2 * h * away) * HALF, HALF), HALF)
        moments[side + h * HALF : side + (h + 1) * HALF, column] = theirs[h]
        moments[column, side + h * HALF : side + (h + 1) * HALF] = theirs[h].T
    few = loadings.shape[0]
    count = test.shape[0] // few
    for ref, at in ((test, 0), (test_other, side)):
        for i in range(count):
            row = pl.multiple_of(at + (samp ^ source(i, count)) * few, few)
            gathered[pl.ds(row, few), :] = ref[i * few : (i + 1) * few, :]
    tests = gathered[...]
    product[...] = dot_pieces(pieces(moments[...]), tests, 1, 0)
    gram = dot_pieces_right(tests, pieces(product[...]), 0, 0)
    inverse_factor(gram, inverse)
    share = basis.shape[0]
    rows = pl.ds(pl.multiple_of(core * share, share), share)
    sketch = dot(standard[rows, :], tests[:side], 1, 0, lax.Precision.DEFAULT) + dot(
        standard_other[rows, :], tests[side:], 1, 0, lax.Precision.DEFAULT
    )
    basis[...] = math.sqrt(total) * dot(sketch, inverse[...], 1, 1)
    own = product[pl.ds(pl.multiple_of(samp * few, few), few), :]
    loadings[...] = dot(own, inverse[...], 1, 1)


def call(kernel, shapes, inputs, place=None, scratch=()):
    vmem = pl.BlockSpec(memory_space=VMEM)
    specs = [vmem] * len(inputs)
    if place is not None:
        specs, inputs = [pl.BlockSpec(memory_space=pltpu.SMEM)] + specs, [place] + list(inputs)
    many = isinstance(shapes, (list, tuple))
    return pl.pallas_call(
        kernel,
        out_shape=shapes,
        in_specs=specs,
        out_specs=[vmem] * len(shapes) if many else vmem,
        scratch_shapes=list(scratch),
        compiler_params=pltpu.CompilerParams(vmem_limit_bytes=24 * 2**20),
    )(*inputs)


def swap(x, axis, bit):
    return lax.ppermute(x, axis, [(i, i ^ bit) for i in range(lax.axis_size(axis))])


def swap_by_core(x, bits):
    pairs = [(2 * i + c, 2 * (i ^ bits[c]) + c) for i in range(lax.axis_size("samp")) for c in range(2)]
    return lax.ppermute(x, ("samp", "mark"), pairs)


def upper(bits):
    mine = jnp.where(lax.axis_index("mark") == 0, bits[0], bits[1])
    return (lax.axis_index("samp") & mine) != 0


def in_order(x, got, up):
    return jnp.where(up, jnp.concatenate([got, x], 0), jnp.concatenate([x, got], 0))


def samp_bits():
    return [1 << i for i in range((lax.axis_size("samp") - 1).bit_length())]


def step_kernel(x, got, blocks, got_blocks, total, joined):
    total[...] = x[...] + got[...]
    joined[: blocks.shape[0], :] = blocks[...]
    joined[blocks.shape[0] :, :] = got_blocks[...]


def sum_plan(count):
    bits = [1 << i for i in range((count - 1).bit_length())]
    if len(bits) < 3:
        return list(zip(bits, bits[::-1]))
    return list(zip(bits[:1] + bits[2:3] + bits[1:2] + bits[3:], bits[2:3] + bits[:1] + bits[3:] + bits[1:2]))


def gather_plan(count):
    return [1 << i for i in reversed(range((count - 1).bit_length()))]


def source(i, count):
    return sum(bit for n, bit in enumerate(gather_plan(count)) if i >> n & 1)


def sum_and_gather(x, test, got_test):
    count = lax.axis_size("samp")
    sums, gathers = sum_plan(count), gather_plan(count)
    half, up = x.shape[0] // 2, upper(sums[0])
    kept = jnp.where(up, x[half:], x[:half])
    sent = jnp.where(up, x[:half], x[half:])
    test = jnp.concatenate([test, got_test], 0)
    for step, pair in enumerate(sums):
        got = swap_by_core(sent, pair)
        if step + 1 < len(gathers):
            got_test = swap(test, "samp", gathers[step + 1])
            kept, test = call(
                step_kernel,
                [
                    jax.ShapeDtypeStruct(kept.shape, kept.dtype),
                    jax.ShapeDtypeStruct((2 * test.shape[0], test.shape[1]), test.dtype),
                ],
                [kept, got, test, got_test],
            )
        else:
            kept = kept + got
        sent = kept
    test_other = swap(test, "mark", 1)
    return in_order(kept, swap_by_core(kept, sums[0]), up), test, test_other


def two_marks(dosage, alt_count, obs_count, sample_weight, test_matrix):
    rows, cols = dosage.shape
    few, rank = test_matrix.shape
    samples = rows * lax.axis_size("samp")
    place = jnp.stack([lax.axis_index("samp"), lax.axis_index("mark")]).astype(jnp.int32)
    standard = call(
        standard_kernel,
        jax.ShapeDtypeStruct((rows, cols), BF16),
        [dosage, alt_count.reshape(1, cols), obs_count.reshape(1, cols), sample_weight.reshape(1, rows)],
    )
    standard_other = swap(standard, "mark", 1)
    got_test = swap(test_matrix, "samp", gather_plan(lax.axis_size("samp"))[0])
    blocks = call(
        moment_kernel,
        jax.ShapeDtypeStruct((5 * HALF, HALF), F32),
        [standard, standard_other],
        place,
    )
    blocks, test, test_other = sum_and_gather(blocks, test_matrix, got_test)
    others = swap(blocks, "mark", 1)
    kernel = lambda *refs: final_kernel(samples, *refs)
    basis, loadings = call(
        kernel,
        [jax.ShapeDtypeStruct((rows // 2, rank), F32), jax.ShapeDtypeStruct((few, rank), F32)],
        [blocks, others, test, test_other, standard, standard_other],
        place,
        [VMEM((2 * cols, 2 * cols), F32), VMEM((rank, rank), F32), VMEM((2 * cols, rank), F32), VMEM((2 * cols, rank), BF16)],
    )
    return basis, loadings


def any_marks(dosage, alt_count, obs_count, sample_weight, test_matrix):
    freq = alt_count.astype(F32) / (2.0 * obs_count.astype(F32))
    scale = 1.0 / jnp.sqrt(2.0 * freq * (1.0 - freq))
    standard = (jnp.sqrt(sample_weight)[:, None] * (dosage.astype(F32) - 2.0 * freq) * scale).astype(BF16)
    rank = test_matrix.shape[1]
    partial_value = jnp.dot(
        standard, lax.all_gather(test_matrix, "samp", axis=0, tiled=True), preferred_element_type=F32
    )
    share = standard.shape[0] // lax.axis_size("mark")
    sketch = lax.psum(partial_value, "mark")
    own_rows = lax.dynamic_slice_in_dim(sketch, lax.axis_index("mark") * share, share, 0)
    gram = dot(sketch, sketch, 0, 0)
    lower = jnp.linalg.cholesky(lax.psum(gram, "samp"))
    inverse = lax.linalg.triangular_solve(lower, jnp.eye(rank, dtype=F32), left_side=True, lower=True)
    basis = math.sqrt(standard.shape[0] * lax.axis_size("samp")) * dot(own_rows, inverse, 1, 1)
    projected = lax.psum_scatter(
        dot(standard, sketch.astype(BF16), 0, 0, lax.Precision.DEFAULT), "samp", scatter_dimension=0, tiled=True
    )
    return basis, dot(projected, inverse, 1, 1)


def solution(mesh):
    samp, mark = mesh.shape["samp"], mesh.shape["mark"]

    def per_device(dosage, *rest):
        fits = mark == 2 and samp >= 4 and samp & (samp - 1) == 0 and dosage.shape[1] == 2 * HALF
        return (two_marks if fits else any_marks)(dosage, *rest)

    return jax.shard_map(
        per_device,
        mesh=mesh,
        in_specs=(P("samp", "mark"), P("mark"), P("mark"), P("samp"), P(("mark", "samp"), None)),
        out_specs=(P(("samp", "mark"), None), P(("mark", "samp"), None)),
        check_vma=False,
    )
```

```python
import math

import jax
import jax.numpy as jnp
from jax import lax
from jax.experimental import pallas as pl
from jax.experimental.pallas import tpu as pltpu
from jax.sharding import PartitionSpec as P

F32, BF16 = jnp.float32, jnp.bfloat16
HALF = 128
BLOCK = 128
VMEM = pltpu.VMEM


def dot(a, b, ca, cb, precision=lax.Precision.HIGHEST):
    return lax.dot_general(
        a, b, (((ca,), (cb,)), ((), ())), precision=precision, preferred_element_type=F32
    )


def pieces(x):
    high = x.astype(BF16)
    rest = x - high.astype(F32)
    mid = rest.astype(BF16)
    return high, mid, (rest - mid.astype(F32)).astype(BF16)


def dot_pieces(parts, b, ca, cb):
    terms = [dot(p, b, ca, cb, lax.Precision.DEFAULT) for p in parts]
    return terms[0] + (terms[1] + terms[2])


def dot_pieces_right(a, parts, ca, cb):
    terms = [dot(a, p, ca, cb, lax.Precision.DEFAULT) for p in parts]
    return terms[0] + (terms[1] + terms[2])


def standard_kernel(dosage, alt, obs, weight, out):
    freq = alt[...].astype(F32) / (2.0 * obs[...].astype(F32))
    scale = 1.0 / jnp.sqrt(2.0 * freq * (1.0 - freq))
    root = jnp.sqrt(weight[...])
    rows, cols = dosage.shape
    for r in range(0, rows, HALF):
        column = jnp.transpose(jnp.broadcast_to(root[:, r : r + HALF], (HALF, HALF)))
        for c in range(0, cols, HALF):
            x = dosage[r : r + HALF, c : c + HALF].astype(F32)
            f = freq[:, c : c + HALF]
            out[r : r + HALF, c : c + HALF] = (column * (x - 2.0 * f) * scale[:, c : c + HALF]).astype(BF16)


def moment_kernel(place, own, other, out):
    core = place[1]
    low, high = own[:, :HALF], own[:, HALF:]
    first = other[:, pl.ds(pl.multiple_of(core * HALF, HALF), HALF)]
    second = other[:, pl.ds(pl.multiple_of((1 - core) * HALF, HALF), HALF)]
    for i, (a, b) in enumerate(((low, low), (high, low), (high, high), (low, first), (high, second))):
        out[i * HALF : (i + 1) * HALF, :] = dot(a, b, 0, 0, lax.Precision.DEFAULT)


def eliminate(groups, slots):
    shape = groups[0].shape
    lane = lax.broadcasted_iota(jnp.int32, shape, 1)
    sub = lax.broadcasted_iota(jnp.int32, shape, 0)
    spread = lambda x: jnp.broadcast_to(x, shape)
    groups, result = list(groups), []
    for g in range(len(groups)):
        j = 8 * g
        columns = lambda group: [
            jnp.take_along_axis(group, jnp.full(shape, j + k, jnp.int32), axis=1) for k in range(8)
        ]
        slot = 9 * (g % 4)
        slots[slot + 8] = groups[g]
        rows = [spread(slots[slot + 8, k : k + 1, :]) for k in range(8)]
        for k, c in enumerate(columns(groups[g])):
            slots[slot + k] = c
        a = {(i, k): spread(slots[slot + k, i : i + 1, :]) for k in range(8) for i in range(k, 8)}
        inside = (lane >= j) & (lane < j + 8)
        root, done, low = [], [], {}
        block = jnp.zeros(shape, F32)
        for k in range(8):
            q = lax.rsqrt(a[k, k])
            root.append(q)
            for i in range(k + 1, 8):
                low[i, k] = a[i, k] * q
            for i in range(k + 1, 8):
                for m in range(k + 1, i + 1):
                    a[i, m] = a[i, m] - low[i, k] * low[m, k]
            row = jnp.where(inside, jnp.where(lane == j + k, 1.0, 0.0), rows[k])
            for m in range(k):
                row = row - low[k, m] * done[m]
            done.append(row * q)
            block = jnp.where((sub == k) & (lane <= j + k), done[k], block)
        result.append(block)
        if g + 1 == len(groups):
            break
        factors = []
        for k, c in enumerate(columns(groups[g + 1])):
            for m in range(k):
                c = c - factors[m] * low[k, m]
            factors.append(c * root[k])
        x = jnp.where(inside, 0.0, groups[g + 1])
        for k in range(8):
            x = x - factors[k] * done[k]
        groups[g + 1] = x
        update = [None] * 8
        for k in reversed(range(8)):
            x = done[k]
            for m in range(k + 1, 8):
                x = x - low[m, k] * update[m]
            update[k] = x * root[k]
        for n in range(g + 2, len(groups)):
            x = jnp.where(inside, 0.0, groups[n])
            for k, c in enumerate(columns(groups[n])):
                x = x - c * update[k]
            groups[n] = x
    return result


def inverse_factor(gram, out, slots):
    n = gram.shape[0]
    rest, corner = gram, gram[:BLOCK, :BLOCK]
    for at in range(0, n, BLOCK):
        end = at + BLOCK
        row = rest[:BLOCK]
        inv = jnp.concatenate(eliminate([corner[i : i + 8, :] for i in range(0, BLOCK, 8)], slots), 0)
        if end == n:
            out[at:end, :] = jnp.concatenate([dot(inv, row[:, :at], 1, 0), inv], 1) if at else inv
            break
        ahead = dot(inv, row[:, end : end + BLOCK], 1, 0)
        corner = rest[BLOCK : 2 * BLOCK, end : end + BLOCK] - dot(ahead, ahead, 0, 0)
        full = dot(inv, row, 1, 0)
        joined = jnp.concatenate(([full[:, :at]] if at else []) + [inv, full[:, end:]], 1)
        lane = lax.broadcasted_iota(jnp.int32, (BLOCK, n), 1)
        out[at:end, :] = jnp.where(lane < end, joined, 0.0)
        below = rest[BLOCK:]
        lane = lax.broadcasted_iota(jnp.int32, below.shape, 1)
        rest = jnp.where((lane >= at) & (lane < end), 0.0, below) - dot(joined[:, end:], joined, 0, 0)


def final_kernel(
    total, place, blocks, others, test, test_other, standard, standard_other, basis, loadings, moments, inverse, product, gathered, slots
):
    samp, core = place[0], place[1]
    side = 2 * HALF
    block = lambda ref, i: ref[i * HALF : (i + 1) * HALF, :]
    for ref, at in ((blocks, 0), (others, side)):
        corner = block(ref, 1)
        moments[at : at + HALF, at : at + HALF] = block(ref, 0)
        moments[at + HALF : at + side, at : at + HALF] = corner
        moments[at : at + HALF, at + HALF : at + side] = corner.T
        moments[at + HALF : at + side, at + HALF : at + side] = block(ref, 2)
    mine, theirs = (block(blocks, 3), block(blocks, 4)), (block(others, 3), block(others, 4))
    for h in range(2):
        column = pl.ds(pl.multiple_of(side + (h + core - 2 * h * core) * HALF, HALF), HALF)
        moments[h * HALF : (h + 1) * HALF, column] = mine[h]
        moments[column, h * HALF : (h + 1) * HALF] = mine[h].T
        away = 1 - core
        column = pl.ds(pl.multiple_of((h + away - 2 * h * away) * HALF, HALF), HALF)
        moments[side + h * HALF : side + (h + 1) * HALF, column] = theirs[h]
        moments[column, side + h * HALF : side + (h + 1) * HALF] = theirs[h].T
    few = loadings.shape[0]
    count = test.shape[0] // few
    for ref, at in ((test, 0), (test_other, side)):
        for i in range(count):
            row = pl.multiple_of(at + (samp ^ source(i, count)) * few, few)
            gathered[pl.ds(row, few), :] = ref[i * few : (i + 1) * few, :]
    tests = gathered[...]
    product[...] = dot_pieces(pieces(moments[...]), tests, 1, 0)
    gram = dot_pieces_right(tests, pieces(product[...]), 0, 0)
    inverse_factor(gram, inverse, slots)
    share = basis.shape[0]
    rows = pl.ds(pl.multiple_of(core * share, share), share)
    sketch = dot(standard[rows, :], tests[:side], 1, 0, lax.Precision.DEFAULT) + dot(
        standard_other[rows, :], tests[side:], 1, 0, lax.Precision.DEFAULT
    )
    basis[...] = math.sqrt(total) * dot(sketch, inverse[...], 1, 1)
    own = product[pl.ds(pl.multiple_of(samp * few, few), few), :]
    loadings[...] = dot(own, inverse[...], 1, 1)


def call(kernel, shapes, inputs, place=None, scratch=()):
    vmem = pl.BlockSpec(memory_space=VMEM)
    specs = [vmem] * len(inputs)
    if place is not None:
        specs, inputs = [pl.BlockSpec(memory_space=pltpu.SMEM)] + specs, [place] + list(inputs)
    many = isinstance(shapes, (list, tuple))
    return pl.pallas_call(
        kernel,
        out_shape=shapes,
        in_specs=specs,
        out_specs=[vmem] * len(shapes) if many else vmem,
        scratch_shapes=list(scratch),
        compiler_params=pltpu.CompilerParams(vmem_limit_bytes=24 * 2**20),
    )(*inputs)


def swap(x, axis, bit):
    return lax.ppermute(x, axis, [(i, i ^ bit) for i in range(lax.axis_size(axis))])


def swap_by_core(x, bits):
    pairs = [(2 * i + c, 2 * (i ^ bits[c]) + c) for i in range(lax.axis_size("samp")) for c in range(2)]
    return lax.ppermute(x, ("samp", "mark"), pairs)


def upper(bits):
    mine = jnp.where(lax.axis_index("mark") == 0, bits[0], bits[1])
    return (lax.axis_index("samp") & mine) != 0


def in_order(x, got, up):
    return jnp.where(up, jnp.concatenate([got, x], 0), jnp.concatenate([x, got], 0))


def samp_bits():
    return [1 << i for i in range((lax.axis_size("samp") - 1).bit_length())]


def step_kernel(x, got, blocks, got_blocks, total, joined):
    total[...] = x[...] + got[...]
    joined[: blocks.shape[0], :] = blocks[...]
    joined[blocks.shape[0] :, :] = got_blocks[...]


def sum_plan(count):
    bits = [1 << i for i in range((count - 1).bit_length())]
    if len(bits) < 3:
        return list(zip(bits, bits[::-1]))
    return list(zip(bits[:1] + bits[2:3] + bits[1:2] + bits[3:], bits[2:3] + bits[:1] + bits[3:] + bits[1:2]))


def gather_plan(count):
    return [1 << i for i in reversed(range((count - 1).bit_length()))]


def source(i, count):
    return sum(bit for n, bit in enumerate(gather_plan(count)) if i >> n & 1)


def sum_and_gather(x, test, got_test):
    count = lax.axis_size("samp")
    sums, gathers = sum_plan(count), gather_plan(count)
    half, up = x.shape[0] // 2, upper(sums[0])
    kept = jnp.where(up, x[half:], x[:half])
    sent = jnp.where(up, x[:half], x[half:])
    test = jnp.concatenate([test, got_test], 0)
    for step, pair in enumerate(sums):
        got = swap_by_core(sent, pair)
        if step + 1 < len(gathers):
            got_test = swap(test, "samp", gathers[step + 1])
            kept, test = call(
                step_kernel,
                [
                    jax.ShapeDtypeStruct(kept.shape, kept.dtype),
                    jax.ShapeDtypeStruct((2 * test.shape[0], test.shape[1]), test.dtype),
                ],
                [kept, got, test, got_test],
            )
        else:
            kept = kept + got
        sent = kept
    test_other = swap(test, "mark", 1)
    return in_order(kept, swap_by_core(kept, sums[0]), up), test, test_other


def two_marks(dosage, alt_count, obs_count, sample_weight, test_matrix):
    rows, cols = dosage.shape
    few, rank = test_matrix.shape
    samples = rows * lax.axis_size("samp")
    place = jnp.stack([lax.axis_index("samp"), lax.axis_index("mark")]).astype(jnp.int32)
    standard = call(
        standard_kernel,
        jax.ShapeDtypeStruct((rows, cols), BF16),
        [dosage, alt_count.reshape(1, cols), obs_count.reshape(1, cols), sample_weight.reshape(1, rows)],
    )
    standard_other = swap(standard, "mark", 1)
    got_test = swap(test_matrix, "samp", gather_plan(lax.axis_size("samp"))[0])
    blocks = call(
        moment_kernel,
        jax.ShapeDtypeStruct((5 * HALF, HALF), F32),
        [standard, standard_other],
        place,
    )
    blocks, test, test_other = sum_and_gather(blocks, test_matrix, got_test)
    others = swap(blocks, "mark", 1)
    kernel = lambda *refs: final_kernel(samples, *refs)
    basis, loadings = call(
        kernel,
        [jax.ShapeDtypeStruct((rows // 2, rank), F32), jax.ShapeDtypeStruct((few, rank), F32)],
        [blocks, others, test, test_other, standard, standard_other],
        place,
        [VMEM((2 * cols, 2 * cols), F32), VMEM((rank, rank), F32), VMEM((2 * cols, rank), F32), VMEM((2 * cols, rank), BF16), VMEM((36, 8, BLOCK), F32)],
    )
    return basis, loadings


def any_marks(dosage, alt_count, obs_count, sample_weight, test_matrix):
    freq = alt_count.astype(F32) / (2.0 * obs_count.astype(F32))
    scale = 1.0 / jnp.sqrt(2.0 * freq * (1.0 - freq))
    standard = (jnp.sqrt(sample_weight)[:, None] * (dosage.astype(F32) - 2.0 * freq) * scale).astype(BF16)
    rank = test_matrix.shape[1]
    partial_value = jnp.dot(
        standard, lax.all_gather(test_matrix, "samp", axis=0, tiled=True), preferred_element_type=F32
    )
    share = standard.shape[0] // lax.axis_size("mark")
    sketch = lax.psum(partial_value, "mark")
    own_rows = lax.dynamic_slice_in_dim(sketch, lax.axis_index("mark") * share, share, 0)
    gram = dot(sketch, sketch, 0, 0)
    lower = jnp.linalg.cholesky(lax.psum(gram, "samp"))
    inverse = lax.linalg.triangular_solve(lower, jnp.eye(rank, dtype=F32), left_side=True, lower=True)
    basis = math.sqrt(standard.shape[0] * lax.axis_size("samp")) * dot(own_rows, inverse, 1, 1)
    projected = lax.psum_scatter(
        dot(standard, sketch.astype(BF16), 0, 0, lax.Precision.DEFAULT), "samp", scatter_dimension=0, tiled=True
    )
    return basis, dot(projected, inverse, 1, 1)


def solution(mesh):
    samp, mark = mesh.shape["samp"], mesh.shape["mark"]

    def per_device(dosage, *rest):
        samples, width = dosage.shape
        few, rank = rest[-1].shape
        fits = mark == 2 and samp >= 4 and samp & (samp - 1) == 0 and width == 2 * HALF
        fits = fits and samples % (2 * HALF) == 0 and rank % BLOCK == 0 and few % 16 == 0
        return (two_marks if fits else any_marks)(dosage, *rest)

    return jax.shard_map(
        per_device,
        mesh=mesh,
        in_specs=(P("samp", "mark"), P("mark"), P("mark"), P("samp"), P(("mark", "samp"), None)),
        out_specs=(P(("samp", "mark"), None), P(("mark", "samp"), None)),
        check_vma=False,
    )
```

```python
import math

import jax
import jax.numpy as jnp
from jax import lax
from jax.experimental import pallas as pl
from jax.experimental.pallas import tpu as pltpu
from jax.sharding import PartitionSpec as P

F32, BF16 = jnp.float32, jnp.bfloat16
HALF = 128
BLOCK = 128
VMEM = pltpu.VMEM


def dot(a, b, ca, cb, precision=lax.Precision.HIGHEST):
    return lax.dot_general(
        a, b, (((ca,), (cb,)), ((), ())), precision=precision, preferred_element_type=F32
    )


def pieces(x):
    high = x.astype(BF16)
    rest = x - high.astype(F32)
    mid = rest.astype(BF16)
    return high, mid, (rest - mid.astype(F32)).astype(BF16)


def dot_pieces(parts, b, ca, cb):
    terms = [dot(p, b, ca, cb, lax.Precision.DEFAULT) for p in parts]
    return terms[0] + (terms[1] + terms[2])


def dot_pieces_right(a, parts, ca, cb):
    terms = [dot(a, p, ca, cb, lax.Precision.DEFAULT) for p in parts]
    return terms[0] + (terms[1] + terms[2])


def standard_kernel(dosage, alt, obs, weight, out):
    freq = alt[...].astype(F32) / (2.0 * obs[...].astype(F32))
    scale = 1.0 / jnp.sqrt(2.0 * freq * (1.0 - freq))
    root = jnp.sqrt(weight[...])
    rows, cols = dosage.shape
    for r in range(0, rows, HALF):
        column = jnp.transpose(jnp.broadcast_to(root[:, r : r + HALF], (HALF, HALF)))
        for c in range(0, cols, HALF):
            x = dosage[r : r + HALF, c : c + HALF].astype(F32)
            f = freq[:, c : c + HALF]
            out[r : r + HALF, c : c + HALF] = (column * (x - 2.0 * f) * scale[:, c : c + HALF]).astype(BF16)


def moment_kernel(own, other, out):
    core = lax.axis_index("mark")
    low, high = own[:, :HALF], own[:, HALF:]
    first = other[:, pl.ds(pl.multiple_of(core * HALF, HALF), HALF)]
    second = other[:, pl.ds(pl.multiple_of((1 - core) * HALF, HALF), HALF)]
    for i, (a, b) in enumerate(((low, low), (high, low), (high, high), (low, first), (high, second))):
        out[i * HALF : (i + 1) * HALF, :] = dot(a, b, 0, 0, lax.Precision.DEFAULT)


def eliminate(groups, slots, factor_slots):
    shape = groups[0].shape
    lane = lax.broadcasted_iota(jnp.int32, shape, 1)
    sub = lax.broadcasted_iota(jnp.int32, shape, 0)
    spread = lambda x: jnp.broadcast_to(x, shape)
    columns = lambda x, j: [jnp.take_along_axis(x, jnp.full(shape, j + k, jnp.int32), axis=1) for k in range(8)]
    groups, result = list(groups), []
    pivots = columns(groups[0], 0)
    for g in range(len(groups)):
        j, last = 8 * g, g + 1 == len(groups)
        slot, factor_slot = 9 * (g % 4), 8 * (g % 4)
        slots[slot + 8] = groups[g]
        rows = [spread(slots[slot + 8, k : k + 1, :]) for k in range(8)]
        for k in range(8):
            slots[slot + k] = pivots[k]
        a = {(i, k): spread(slots[slot + k, i : i + 1, :]) for k in range(8) for i in range(k, 8)}
        inside = (lane >= j) & (lane < j + 8)
        root, done, low, factors = [], [], {}, []
        block = jnp.zeros(shape, F32)
        if not last:
            left = columns(groups[g + 1], j)
            pivots = columns(groups[g + 1], j + 8)
            ahead = jnp.where(inside, 0.0, groups[g + 1])
        for k in range(8):
            q = lax.rsqrt(a[k, k])
            root.append(q)
            for i in range(k + 1, 8):
                low[i, k] = a[i, k] * q
            for i in range(k + 1, 8):
                for m in range(k + 1, i + 1):
                    a[i, m] = a[i, m] - low[i, k] * low[m, k]
            row = jnp.where(inside, jnp.where(lane == j + k, 1.0, 0.0), rows[k])
            for m in range(k):
                row = row - low[k, m] * done[m]
            done.append(row * q)
            block = jnp.where((sub == k) & (lane <= j + k), done[k], block)
            if not last:
                c = left[k]
                for m in range(k):
                    c = c - factors[m] * low[k, m]
                factors.append(c * q)
                factor_slots[factor_slot + k] = factors[k]
                for i in range(8):
                    pivots[i] = pivots[i] - factors[k] * spread(factor_slots[factor_slot + k, i : i + 1, :])
                ahead = ahead - factors[k] * done[k]
        result.append(block)
        if last:
            break
        groups[g + 1] = ahead
        update = [None] * 8
        for k in reversed(range(8)):
            x = done[k]
            for m in range(k + 1, 8):
                x = x - low[m, k] * update[m]
            update[k] = x * root[k]
        for n in range(g + 2, len(groups)):
            x = jnp.where(inside, 0.0, groups[n])
            for k, c in enumerate(columns(groups[n], j)):
                x = x - c * update[k]
            groups[n] = x
    return result


def inverse_factor(gram, out, ready, *slots):
    n = gram.shape[0]
    rest, corner = gram, gram[:BLOCK, :BLOCK]
    for at in range(0, n, BLOCK):
        end = at + BLOCK
        row = rest[:BLOCK]
        inv = jnp.concatenate(eliminate([corner[i : i + 8, :] for i in range(0, BLOCK, 8)], *slots), 0)
        if end == n:
            out[at:end, :] = jnp.concatenate([dot(inv, row[:, :at], 1, 0), inv], 1) if at else inv
            ready(at, end)
            break
        ahead = dot(inv, row[:, end : end + BLOCK], 1, 0)
        corner = rest[BLOCK : 2 * BLOCK, end : end + BLOCK] - dot(ahead, ahead, 0, 0)
        full = dot(inv, row, 1, 0)
        joined = jnp.concatenate(([full[:, :at]] if at else []) + [inv, full[:, end:]], 1)
        lane = lax.broadcasted_iota(jnp.int32, (BLOCK, n), 1)
        out[at:end, :] = jnp.where(lane < end, joined, 0.0)
        ready(at, end)
        below = rest[BLOCK:]
        lane = lax.broadcasted_iota(jnp.int32, below.shape, 1)
        rest = jnp.where((lane >= at) & (lane < end), 0.0, below) - dot(joined[:, end:], joined, 0, 0)


def final_kernel(
    total, blocks, others, test, test_other, standard, standard_other, basis, loadings, moments, inverse, product, gathered, *slots
):
    samp, core = lax.axis_index("samp"), lax.axis_index("mark")
    side = 2 * HALF
    block = lambda ref, i: ref[i * HALF : (i + 1) * HALF, :]
    for ref, at in ((blocks, 0), (others, side)):
        corner = block(ref, 1)
        moments[at : at + HALF, at : at + HALF] = block(ref, 0)
        moments[at + HALF : at + side, at : at + HALF] = corner
        moments[at : at + HALF, at + HALF : at + side] = corner.T
        moments[at + HALF : at + side, at + HALF : at + side] = block(ref, 2)
    mine, theirs = (block(blocks, 3), block(blocks, 4)), (block(others, 3), block(others, 4))
    for h in range(2):
        column = pl.ds(pl.multiple_of(side + (h + core - 2 * h * core) * HALF, HALF), HALF)
        moments[h * HALF : (h + 1) * HALF, column] = mine[h]
        moments[column, h * HALF : (h + 1) * HALF] = mine[h].T
        away = 1 - core
        column = pl.ds(pl.multiple_of((h + away - 2 * h * away) * HALF, HALF), HALF)
        moments[side + h * HALF : side + (h + 1) * HALF, column] = theirs[h]
        moments[column, side + h * HALF : side + (h + 1) * HALF] = theirs[h].T
    few = loadings.shape[0]
    count = test.shape[0] // few
    for ref, at in ((test, 0), (test_other, side)):
        for i in range(count):
            row = pl.multiple_of(at + (samp ^ source(i, count)) * few, few)
            gathered[pl.ds(row, few), :] = ref[i * few : (i + 1) * few, :]
    tests = gathered[...]
    product[...] = dot_pieces(pieces(moments[...]), tests, 1, 0)
    gram = dot_pieces_right(tests, pieces(product[...]), 0, 0)
    share = basis.shape[0]
    rows = pl.ds(pl.multiple_of(core * share, share), share)
    sketch = dot(standard[rows, :], tests[:side], 1, 0, lax.Precision.DEFAULT) + dot(
        standard_other[rows, :], tests[side:], 1, 0, lax.Precision.DEFAULT
    )
    sketch_high, sketch_mid, _ = pieces(math.sqrt(total) * sketch)
    few = loadings.shape[0]
    own = product[pl.ds(pl.multiple_of(samp * few, few), few), :]

    def ready(at, end):
        high, mid, _ = pieces(inverse[at:end, :end])
        once = lambda a, b: dot(a[:, :end], b, 1, 1, lax.Precision.DEFAULT)
        basis[:, at:end] = once(sketch_high, high) + (once(sketch_high, mid) + once(sketch_mid, high))
        loadings[:, at:end] = dot(own[:, :end], inverse[at:end, :end], 1, 1)

    inverse_factor(gram, inverse, ready, *slots)


def call(kernel, shapes, inputs, scratch=()):
    vmem = pl.BlockSpec(memory_space=VMEM)
    many = isinstance(shapes, (list, tuple))
    return pl.pallas_call(
        kernel,
        out_shape=shapes,
        in_specs=[vmem] * len(inputs),
        out_specs=[vmem] * len(shapes) if many else vmem,
        scratch_shapes=list(scratch),
        compiler_params=pltpu.CompilerParams(vmem_limit_bytes=24 * 2**20),
    )(*inputs)


def swap(x, axis, bit):
    return lax.ppermute(x, axis, [(i, i ^ bit) for i in range(lax.axis_size(axis))])


def swap_by_core(x, bits):
    pairs = [(2 * i + c, 2 * (i ^ bits[c]) + c) for i in range(lax.axis_size("samp")) for c in range(2)]
    return lax.ppermute(x, ("samp", "mark"), pairs)


def upper(bits):
    mine = jnp.where(lax.axis_index("mark") == 0, bits[0], bits[1])
    return (lax.axis_index("samp") & mine) != 0


def in_order(x, got, up):
    return jnp.where(up, jnp.concatenate([got, x], 0), jnp.concatenate([x, got], 0))


def samp_bits():
    return [1 << i for i in range((lax.axis_size("samp") - 1).bit_length())]


def step_kernel(x, got, blocks, got_blocks, total, joined):
    total[...] = x[...] + got[...]
    joined[: blocks.shape[0], :] = blocks[...]
    joined[blocks.shape[0] :, :] = got_blocks[...]


def sum_plan(count):
    bits = [1 << i for i in range((count - 1).bit_length())]
    return list(zip(bits[:1] + bits[2:3] + bits[1:2] + bits[3:], bits))


def gather_plan(count):
    return [1 << i for i in reversed(range((count - 1).bit_length()))]


def source(i, count):
    return sum(bit for n, bit in enumerate(gather_plan(count)) if i >> n & 1)


def sum_and_gather(x, test, got_test):
    count = lax.axis_size("samp")
    sums, gathers = sum_plan(count), gather_plan(count)
    half, up = x.shape[0] // 2, upper(sums[0])
    kept = jnp.where(up, x[half:], x[:half])
    sent = jnp.where(up, x[:half], x[half:])
    test = jnp.concatenate([test, got_test], 0)
    for step, pair in enumerate(sums):
        got = swap_by_core(sent, pair)
        if step + 1 < len(gathers):
            got_test = swap(test, "samp", gathers[step + 1])
            kept, test = call(
                step_kernel,
                [
                    jax.ShapeDtypeStruct(kept.shape, kept.dtype),
                    jax.ShapeDtypeStruct((2 * test.shape[0], test.shape[1]), test.dtype),
                ],
                [kept, got, test, got_test],
            )
        else:
            kept = kept + got
        sent = kept
    test_other = swap(test, "mark", 1)
    got = swap_by_core(kept, sums[0])
    kept_other = swap(kept, "mark", 1)
    return in_order(kept, got, up), in_order(kept_other, swap(got, "mark", 1), up), test, test_other


def two_marks(dosage, alt_count, obs_count, sample_weight, test_matrix):
    rows, cols = dosage.shape
    few, rank = test_matrix.shape
    samples = rows * lax.axis_size("samp")
    standard = call(
        standard_kernel,
        jax.ShapeDtypeStruct((rows, cols), BF16),
        [dosage, alt_count.reshape(1, cols), obs_count.reshape(1, cols), sample_weight.reshape(1, rows)],
    )
    standard_other = swap(standard, "mark", 1)
    got_test = swap(test_matrix, "samp", gather_plan(lax.axis_size("samp"))[0])
    blocks = call(moment_kernel, jax.ShapeDtypeStruct((5 * HALF, HALF), F32), [standard, standard_other])
    blocks, others, test, test_other = sum_and_gather(blocks, test_matrix, got_test)
    kernel = lambda *refs: final_kernel(samples, *refs)
    basis, loadings = call(
        kernel,
        [jax.ShapeDtypeStruct((rows // 2, rank), F32), jax.ShapeDtypeStruct((few, rank), F32)],
        [blocks, others, test, test_other, standard, standard_other],
        [VMEM((2 * cols, 2 * cols), F32), VMEM((rank, rank), F32), VMEM((2 * cols, rank), F32), VMEM((2 * cols, rank), BF16), VMEM((36, 8, BLOCK), F32), VMEM((32, 8, BLOCK), F32)],
    )
    return basis, loadings


def any_marks(dosage, alt_count, obs_count, sample_weight, test_matrix):
    freq = alt_count.astype(F32) / (2.0 * obs_count.astype(F32))
    scale = 1.0 / jnp.sqrt(2.0 * freq * (1.0 - freq))
    standard = (jnp.sqrt(sample_weight)[:, None] * (dosage.astype(F32) - 2.0 * freq) * scale).astype(BF16)
    rank = test_matrix.shape[1]
    partial_value = jnp.dot(
        standard, lax.all_gather(test_matrix, "samp", axis=0, tiled=True), preferred_element_type=F32
    )
    share = standard.shape[0] // lax.axis_size("mark")
    sketch = lax.psum(partial_value, "mark")
    own_rows = lax.dynamic_slice_in_dim(sketch, lax.axis_index("mark") * share, share, 0)
    gram = dot(sketch, sketch, 0, 0)
    lower = jnp.linalg.cholesky(lax.psum(gram, "samp"))
    inverse = lax.linalg.triangular_solve(lower, jnp.eye(rank, dtype=F32), left_side=True, lower=True)
    basis = math.sqrt(standard.shape[0] * lax.axis_size("samp")) * dot(own_rows, inverse, 1, 1)
    projected = lax.psum_scatter(
        dot(standard, sketch.astype(BF16), 0, 0, lax.Precision.DEFAULT), "samp", scatter_dimension=0, tiled=True
    )
    return basis, dot(projected, inverse, 1, 1)


def solution(mesh):
    samp, mark = mesh.shape["samp"], mesh.shape["mark"]

    def per_device(dosage, *rest):
        samples, width = dosage.shape
        few, rank = rest[-1].shape
        fits = mark == 2 and samp >= 4 and samp & (samp - 1) == 0 and width == 2 * HALF
        fits = fits and samples % (2 * HALF) == 0 and rank % BLOCK == 0 and few % 16 == 0
        return (two_marks if fits else any_marks)(dosage, *rest)

    return jax.shard_map(
        per_device,
        mesh=mesh,
        in_specs=(P("samp", "mark"), P("mark"), P("mark"), P("samp"), P(("mark", "samp"), None)),
        out_specs=(P(("samp", "mark"), None), P(("mark", "samp"), None)),
        check_vma=False,
    )
```

```python
import math

import jax
import jax.numpy as jnp
from jax import lax
from jax.experimental import pallas as pl
from jax.experimental.pallas import tpu as pltpu
from jax.sharding import PartitionSpec as P

F32, BF16 = jnp.float32, jnp.bfloat16
HALF = 128
SQUARE = HALF // 2
BLOCK = 128
VMEM = pltpu.VMEM


def dot(a, b, ca, cb, precision=lax.Precision.HIGHEST):
    return lax.dot_general(
        a, b, (((ca,), (cb,)), ((), ())), precision=precision, preferred_element_type=F32
    )


def pieces(x):
    high = x.astype(BF16)
    rest = x - high.astype(F32)
    mid = rest.astype(BF16)
    return high, mid, (rest - mid.astype(F32)).astype(BF16)


def dot_pieces(parts, b, ca, cb):
    terms = [dot(p, b, ca, cb, lax.Precision.DEFAULT) for p in parts]
    return terms[0] + (terms[1] + terms[2])


def dot_pieces_right(a, parts, ca, cb):
    terms = [dot(a, p, ca, cb, lax.Precision.DEFAULT) for p in parts]
    return terms[0] + (terms[1] + terms[2])


def standard_kernel(dosage, alt, obs, weight, out):
    freq = alt[...].astype(F32) / (2.0 * obs[...].astype(F32))
    scale = 1.0 / jnp.sqrt(2.0 * freq * (1.0 - freq))
    root = jnp.sqrt(weight[...])
    rows, cols = dosage.shape
    for r in range(0, rows, HALF):
        column = jnp.transpose(jnp.broadcast_to(root[:, r : r + HALF], (HALF, HALF)))
        for c in range(0, cols, HALF):
            x = dosage[r : r + HALF, c : c + HALF].astype(F32)
            f = freq[:, c : c + HALF]
            out[r : r + HALF, c : c + HALF] = (column * (x - 2.0 * f) * scale[:, c : c + HALF]).astype(BF16)


def moment_kernel(own, other, out):
    core = lax.axis_index("mark")
    low, high = own[:, :HALF], own[:, HALF:]
    first = other[:, pl.ds(pl.multiple_of(core * HALF, HALF), HALF)]
    second = other[:, pl.ds(pl.multiple_of((1 - core) * HALF, HALF), HALF)]
    for i, (a, b) in enumerate(((high, low), (low, first), (high, second))):
        out[i * HALF : (i + 1) * HALF, :] = dot(a, b, 0, 0, lax.Precision.DEFAULT)
    squares = [dot(a, a, 0, 0, lax.Precision.DEFAULT) for a in (low, high)]
    at = 3 * HALF
    for x in [x[SQUARE:] for x in squares] + [jnp.concatenate([x[:SQUARE, :SQUARE] for x in squares], 1)]:
        out[at : at + SQUARE, :] = x
        at += SQUARE


def eliminate(groups, slots, factor_slots):
    shape = groups[0].shape
    lane = lax.broadcasted_iota(jnp.int32, shape, 1)
    sub = lax.broadcasted_iota(jnp.int32, shape, 0)
    spread = lambda x: jnp.broadcast_to(x, shape)
    columns = lambda x, j: [jnp.take_along_axis(x, jnp.full(shape, j + k, jnp.int32), axis=1) for k in range(8)]
    groups, result = list(groups), []
    pivots = columns(groups[0], 0)
    for g in range(len(groups)):
        j, last = 8 * g, g + 1 == len(groups)
        slot, factor_slot = 9 * (g % 4), 8 * (g % 4)
        slots[slot + 8] = groups[g]
        rows = [spread(slots[slot + 8, k : k + 1, :]) for k in range(8)]
        for k in range(8):
            slots[slot + k] = pivots[k]
        a = {(i, k): spread(slots[slot + k, i : i + 1, :]) for k in range(8) for i in range(k, 8)}
        inside = (lane >= j) & (lane < j + 8)
        root, done, low, factors = [], [], {}, []
        block = jnp.zeros(shape, F32)
        if not last:
            left = columns(groups[g + 1], j)
            pivots = columns(groups[g + 1], j + 8)
            ahead = jnp.where(inside, 0.0, groups[g + 1])
        for k in range(8):
            q = lax.rsqrt(a[k, k])
            root.append(q)
            for i in range(k + 1, 8):
                low[i, k] = a[i, k] * q
            for i in range(k + 1, 8):
                for m in range(k + 1, i + 1):
                    a[i, m] = a[i, m] - low[i, k] * low[m, k]
            row = jnp.where(inside, jnp.where(lane == j + k, 1.0, 0.0), rows[k])
            for m in range(k):
                row = row - low[k, m] * done[m]
            done.append(row * q)
            block = jnp.where((sub == k) & (lane <= j + k), done[k], block)
            if not last:
                c = left[k]
                for m in range(k):
                    c = c - factors[m] * low[k, m]
                factors.append(c * q)
                factor_slots[factor_slot + k] = factors[k]
                for i in range(8):
                    pivots[i] = pivots[i] - factors[k] * spread(factor_slots[factor_slot + k, i : i + 1, :])
                ahead = ahead - factors[k] * done[k]
        result.append(block)
        if last:
            break
        groups[g + 1] = ahead
        update = [None] * 8
        for k in reversed(range(8)):
            x = done[k]
            for m in range(k + 1, 8):
                x = x - low[m, k] * update[m]
            update[k] = x * root[k]
        for n in range(g + 2, len(groups)):
            x = jnp.where(inside, 0.0, groups[n])
            for k, c in enumerate(columns(groups[n], j)):
                x = x - c * update[k]
            groups[n] = x
    return result


def inverse_factor(gram, out, ready, *slots):
    n = gram.shape[0]
    rest, corner = gram, gram[:BLOCK, :BLOCK]
    for at in range(0, n, BLOCK):
        end = at + BLOCK
        row = rest[:BLOCK]
        inv = jnp.concatenate(eliminate([corner[i : i + 8, :] for i in range(0, BLOCK, 8)], *slots), 0)
        if end == n:
            out[at:end, :] = jnp.concatenate([dot(inv, row[:, :at], 1, 0), inv], 1) if at else inv
            ready(at, end)
            break
        ahead = dot(inv, row[:, end : end + BLOCK], 1, 0)
        corner = rest[BLOCK : 2 * BLOCK, end : end + BLOCK] - dot(ahead, ahead, 0, 0)
        full = dot(inv, row, 1, 0)
        joined = jnp.concatenate(([full[:, :at]] if at else []) + [inv, full[:, end:]], 1)
        lane = lax.broadcasted_iota(jnp.int32, (BLOCK, n), 1)
        out[at:end, :] = jnp.where(lane < end, joined, 0.0)
        ready(at, end)
        below = rest[BLOCK:]
        lane = lax.broadcasted_iota(jnp.int32, below.shape, 1)
        rest = jnp.where((lane >= at) & (lane < end), 0.0, below) - dot(joined[:, end:], joined, 0, 0)


def final_kernel(
    total, blocks, others, test, test_other, standard, standard_other, basis, loadings, moments, inverse, product, gathered, *slots
):
    samp, core = lax.axis_index("samp"), lax.axis_index("mark")
    side = 2 * HALF
    block = lambda ref, i: ref[i * HALF : (i + 1) * HALF, :]
    for ref, at in ((blocks, 0), (others, side)):
        corner = block(ref, 0)
        moments[at + HALF : at + side, at : at + HALF] = corner
        moments[at : at + HALF, at + HALF : at + side] = corner.T
        firsts = ref[3 * HALF + 2 * SQUARE :, :]
        for h in range(2):
            lower = ref[3 * HALF + h * SQUARE : 3 * HALF + (h + 1) * SQUARE, :]
            top, columns = at + h * HALF, slice(at + h * HALF, at + (h + 1) * HALF)
            moments[top : top + SQUARE, columns] = jnp.concatenate(
                [firsts[:, h * SQUARE : (h + 1) * SQUARE], lower[:, :SQUARE].T], 1
            )
            moments[top + SQUARE : top + HALF, columns] = lower
    mine, theirs = (block(blocks, 1), block(blocks, 2)), (block(others, 1), block(others, 2))
    for h in range(2):
        column = pl.ds(pl.multiple_of(side + (h + core - 2 * h * core) * HALF, HALF), HALF)
        moments[h * HALF : (h + 1) * HALF, column] = mine[h]
        moments[column, h * HALF : (h + 1) * HALF] = mine[h].T
        away = 1 - core
        column = pl.ds(pl.multiple_of((h + away - 2 * h * away) * HALF, HALF), HALF)
        moments[side + h * HALF : side + (h + 1) * HALF, column] = theirs[h]
        moments[column, side + h * HALF : side + (h + 1) * HALF] = theirs[h].T
    few = loadings.shape[0]
    count = test.shape[0] // few
    for ref, at in ((test, 0), (test_other, side)):
        for i in range(count):
            row = pl.multiple_of(at + (samp ^ source(i, count)) * few, few)
            gathered[pl.ds(row, few), :] = ref[i * few : (i + 1) * few, :]
    tests = gathered[...]
    product[...] = dot_pieces(pieces(moments[...]), tests, 1, 0)
    gram = dot_pieces_right(tests, pieces(product[...]), 0, 0)
    share = basis.shape[0]
    rows = pl.ds(pl.multiple_of(core * share, share), share)
    sketch = dot(standard[rows, :], tests[:side], 1, 0, lax.Precision.DEFAULT) + dot(
        standard_other[rows, :], tests[side:], 1, 0, lax.Precision.DEFAULT
    )
    sketch_high, sketch_mid, _ = pieces(math.sqrt(total) * sketch)
    few = loadings.shape[0]
    own = product[pl.ds(pl.multiple_of(samp * few, few), few), :]

    def ready(at, end):
        high, mid, _ = pieces(inverse[at:end, :end])
        once = lambda a, b: dot(a[:, :end], b, 1, 1, lax.Precision.DEFAULT)
        basis[:, at:end] = once(sketch_high, high) + (once(sketch_high, mid) + once(sketch_mid, high))
        loadings[:, at:end] = dot(own[:, :end], inverse[at:end, :end], 1, 1)

    inverse_factor(gram, inverse, ready, *slots)


def call(kernel, shapes, inputs, scratch=()):
    vmem = pl.BlockSpec(memory_space=VMEM)
    many = isinstance(shapes, (list, tuple))
    return pl.pallas_call(
        kernel,
        out_shape=shapes,
        in_specs=[vmem] * len(inputs),
        out_specs=[vmem] * len(shapes) if many else vmem,
        scratch_shapes=list(scratch),
        compiler_params=pltpu.CompilerParams(vmem_limit_bytes=24 * 2**20),
    )(*inputs)


def swap(x, axis, bit):
    return lax.ppermute(x, axis, [(i, i ^ bit) for i in range(lax.axis_size(axis))])


def swap_by_core(x, bits):
    pairs = [(2 * i + c, 2 * (i ^ bits[c]) + c) for i in range(lax.axis_size("samp")) for c in range(2)]
    return lax.ppermute(x, ("samp", "mark"), pairs)


def upper(bits):
    mine = jnp.where(lax.axis_index("mark") == 0, bits[0], bits[1])
    return (lax.axis_index("samp") & mine) != 0


def in_order(x, got, up):
    return jnp.where(up, jnp.concatenate([got, x], 0), jnp.concatenate([x, got], 0))


def samp_bits():
    return [1 << i for i in range((lax.axis_size("samp") - 1).bit_length())]


def step_kernel(x, got, blocks, got_blocks, total, joined):
    total[...] = x[...] + got[...]
    joined[: blocks.shape[0], :] = blocks[...]
    joined[blocks.shape[0] :, :] = got_blocks[...]


def sum_plan(count):
    bits = [1 << i for i in range((count - 1).bit_length())]
    return list(zip(bits[:1] + bits[2:3] + bits[1:2] + bits[3:], bits))


def gather_plan(count):
    return [1 << i for i in reversed(range((count - 1).bit_length()))]


def source(i, count):
    return sum(bit for n, bit in enumerate(gather_plan(count)) if i >> n & 1)


def sum_and_gather(x, test, got_test):
    count = lax.axis_size("samp")
    sums, gathers = sum_plan(count), gather_plan(count)
    half, up = x.shape[0] // 2, upper(sums[0])
    kept = jnp.where(up, x[half:], x[:half])
    sent = jnp.where(up, x[:half], x[half:])
    test = jnp.concatenate([test, got_test], 0)
    for step, pair in enumerate(sums):
        got = swap_by_core(sent, pair)
        if step + 1 < len(gathers):
            got_test = swap(test, "samp", gathers[step + 1])
            kept, test = call(
                step_kernel,
                [
                    jax.ShapeDtypeStruct(kept.shape, kept.dtype),
                    jax.ShapeDtypeStruct((2 * test.shape[0], test.shape[1]), test.dtype),
                ],
                [kept, got, test, got_test],
            )
        else:
            kept = kept + got
        sent = kept
    test_other = swap(test, "mark", 1)
    got = swap_by_core(kept, sums[0])
    kept_other = swap(kept, "mark", 1)
    return in_order(kept, got, up), in_order(kept_other, swap(got, "mark", 1), up), test, test_other


def two_marks(dosage, alt_count, obs_count, sample_weight, test_matrix):
    rows, cols = dosage.shape
    few, rank = test_matrix.shape
    samples = rows * lax.axis_size("samp")
    standard = call(
        standard_kernel,
        jax.ShapeDtypeStruct((rows, cols), BF16),
        [dosage, alt_count.reshape(1, cols), obs_count.reshape(1, cols), sample_weight.reshape(1, rows)],
    )
    standard_other = swap(standard, "mark", 1)
    got_test = swap(test_matrix, "samp", gather_plan(lax.axis_size("samp"))[0])
    blocks = call(moment_kernel, jax.ShapeDtypeStruct((3 * HALF + 3 * SQUARE, HALF), F32), [standard, standard_other])
    blocks, others, test, test_other = sum_and_gather(blocks, test_matrix, got_test)
    kernel = lambda *refs: final_kernel(samples, *refs)
    basis, loadings = call(
        kernel,
        [jax.ShapeDtypeStruct((rows // 2, rank), F32), jax.ShapeDtypeStruct((few, rank), F32)],
        [blocks, others, test, test_other, standard, standard_other],
        [VMEM((2 * cols, 2 * cols), F32), VMEM((rank, rank), F32), VMEM((2 * cols, rank), F32), VMEM((2 * cols, rank), BF16), VMEM((36, 8, BLOCK), F32), VMEM((32, 8, BLOCK), F32)],
    )
    return basis, loadings


def any_marks(dosage, alt_count, obs_count, sample_weight, test_matrix):
    freq = alt_count.astype(F32) / (2.0 * obs_count.astype(F32))
    scale = 1.0 / jnp.sqrt(2.0 * freq * (1.0 - freq))
    standard = (jnp.sqrt(sample_weight)[:, None] * (dosage.astype(F32) - 2.0 * freq) * scale).astype(BF16)
    rank = test_matrix.shape[1]
    partial_value = jnp.dot(
        standard, lax.all_gather(test_matrix, "samp", axis=0, tiled=True), preferred_element_type=F32
    )
    share = standard.shape[0] // lax.axis_size("mark")
    sketch = lax.psum(partial_value, "mark")
    own_rows = lax.dynamic_slice_in_dim(sketch, lax.axis_index("mark") * share, share, 0)
    gram = dot(sketch, sketch, 0, 0)
    lower = jnp.linalg.cholesky(lax.psum(gram, "samp"))
    inverse = lax.linalg.triangular_solve(lower, jnp.eye(rank, dtype=F32), left_side=True, lower=True)
    basis = math.sqrt(standard.shape[0] * lax.axis_size("samp")) * dot(own_rows, inverse, 1, 1)
    projected = lax.psum_scatter(
        dot(standard, sketch.astype(BF16), 0, 0, lax.Precision.DEFAULT), "samp", scatter_dimension=0, tiled=True
    )
    return basis, dot(projected, inverse, 1, 1)


def solution(mesh):
    samp, mark = mesh.shape["samp"], mesh.shape["mark"]

    def per_device(dosage, *rest):
        samples, width = dosage.shape
        few, rank = rest[-1].shape
        fits = mark == 2 and samp >= 4 and samp & (samp - 1) == 0 and width == 2 * HALF
        fits = fits and samples % (2 * HALF) == 0 and rank % BLOCK == 0 and few % 16 == 0
        return (two_marks if fits else any_marks)(dosage, *rest)

    return jax.shard_map(
        per_device,
        mesh=mesh,
        in_specs=(P("samp", "mark"), P("mark"), P("mark"), P("samp"), P(("mark", "samp"), None)),
        out_specs=(P(("samp", "mark"), None), P(("mark", "samp"), None)),
        check_vma=False,
    )
```

```python
import math

import jax
import jax.numpy as jnp
from jax import lax
from jax.experimental import pallas as pl
from jax.experimental.pallas import tpu as pltpu
from jax.sharding import PartitionSpec as P

F32, BF16 = jnp.float32, jnp.bfloat16
HALF = 128
SQUARE = HALF // 2
BLOCK = 128
VMEM = pltpu.VMEM


def dot(a, b, ca, cb, precision=lax.Precision.HIGHEST):
    return lax.dot_general(
        a, b, (((ca,), (cb,)), ((), ())), precision=precision, preferred_element_type=F32
    )


def pieces(x):
    high = x.astype(BF16)
    rest = x - high.astype(F32)
    mid = rest.astype(BF16)
    return high, mid, (rest - mid.astype(F32)).astype(BF16)


def dot_pieces(parts, b, ca, cb):
    terms = [dot(p, b, ca, cb, lax.Precision.DEFAULT) for p in parts]
    return terms[0] + (terms[1] + terms[2])


def dot_pieces_right(a, parts, ca, cb):
    terms = [dot(a, p, ca, cb, lax.Precision.DEFAULT) for p in parts]
    return terms[0] + (terms[1] + terms[2])


def standard_kernel(dosage, alt, obs, weight, out):
    freq = alt[...].astype(F32) / (2.0 * obs[...].astype(F32))
    scale = 1.0 / jnp.sqrt(2.0 * freq * (1.0 - freq))
    root = jnp.sqrt(weight[...])
    rows, cols = dosage.shape
    for r in range(0, rows, HALF):
        column = jnp.transpose(jnp.broadcast_to(root[:, r : r + HALF], (HALF, HALF)))
        for c in range(0, cols, HALF):
            x = dosage[r : r + HALF, c : c + HALF].astype(F32)
            f = freq[:, c : c + HALF]
            out[r : r + HALF, c : c + HALF] = (column * (x - 2.0 * f) * scale[:, c : c + HALF]).astype(BF16)


def moment_kernel(own, other, out):
    core = lax.axis_index("mark")
    low, high = own[:, :HALF], own[:, HALF:]
    first = other[:, pl.ds(pl.multiple_of(core * HALF, HALF), HALF)]
    second = other[:, pl.ds(pl.multiple_of((1 - core) * HALF, HALF), HALF)]
    for i, (a, b) in enumerate(((high, low), (low, first), (high, second))):
        out[i * HALF : (i + 1) * HALF, :] = dot(a, b, 0, 0, lax.Precision.DEFAULT)
    squares = [dot(a, a, 0, 0, lax.Precision.DEFAULT) for a in (low, high)]
    at = 3 * HALF
    for x in [x[SQUARE:] for x in squares] + [jnp.concatenate([x[:SQUARE, :SQUARE] for x in squares], 1)]:
        out[at : at + SQUARE, :] = x
        at += SQUARE


def eliminate(groups, slots, factor_slots):
    shape = groups[0].shape
    lane = lax.broadcasted_iota(jnp.int32, shape, 1)
    sub = lax.broadcasted_iota(jnp.int32, shape, 0)
    spread = lambda x: jnp.broadcast_to(x, shape)
    columns = lambda x, j: [jnp.take_along_axis(x, jnp.full(shape, j + k, jnp.int32), axis=1) for k in range(8)]
    groups, result = list(groups), []
    pivots = columns(groups[0], 0)
    for g in range(len(groups)):
        j, last = 8 * g, g + 1 == len(groups)
        slot, factor_slot = 9 * (g % 4), 8 * (g % 4)
        slots[slot + 8] = groups[g]
        rows = [spread(slots[slot + 8, k : k + 1, :]) for k in range(8)]
        for k in range(8):
            slots[slot + k] = pivots[k]
        a = {(i, k): spread(slots[slot + k, i : i + 1, :]) for k in range(8) for i in range(k, 8)}
        inside = (lane >= j) & (lane < j + 8)
        root, done, low, factors = [], [], {}, []
        block = jnp.zeros(shape, F32)
        if not last:
            left = columns(groups[g + 1], j)
            pivots = columns(groups[g + 1], j + 8)
            ahead = jnp.where(inside, 0.0, groups[g + 1])
        for k in range(8):
            q = lax.rsqrt(a[k, k])
            root.append(q)
            for i in range(k + 1, 8):
                low[i, k] = a[i, k] * q
            for i in range(k + 1, 8):
                for m in range(k + 1, i + 1):
                    a[i, m] = a[i, m] - low[i, k] * low[m, k]
            row = jnp.where(inside, jnp.where(lane == j + k, 1.0, 0.0), rows[k])
            for m in range(k):
                row = row - low[k, m] * done[m]
            done.append(row * q)
            block = jnp.where((sub == k) & (lane <= j + k), done[k], block)
            if not last:
                c = left[k]
                for m in range(k):
                    c = c - factors[m] * low[k, m]
                factors.append(c * q)
                factor_slots[factor_slot + k] = factors[k]
                for i in range(8):
                    pivots[i] = pivots[i] - factors[k] * spread(factor_slots[factor_slot + k, i : i + 1, :])
                ahead = ahead - factors[k] * done[k]
        result.append(block)
        if last:
            break
        groups[g + 1] = ahead
        update = [None] * 8
        for k in reversed(range(8)):
            x = done[k]
            for m in range(k + 1, 8):
                x = x - low[m, k] * update[m]
            update[k] = x * root[k]
        for n in range(g + 2, len(groups)):
            x = jnp.where(inside, 0.0, groups[n])
            for k, c in enumerate(columns(groups[n], j)):
                x = x - c * update[k]
            groups[n] = x
    return result


def inverse_factor(gram, out, ready, *slots):
    n = gram.shape[0]
    rest, corner = gram, gram[:BLOCK, :BLOCK]
    for at in range(0, n, BLOCK):
        end = at + BLOCK
        row = rest[:BLOCK]
        inv = jnp.concatenate(eliminate([corner[i : i + 8, :] for i in range(0, BLOCK, 8)], *slots), 0)
        if end == n:
            out[at:end, :] = jnp.concatenate([dot(inv, row[:, :at], 1, 0), inv], 1) if at else inv
            ready(at, end)
            break
        ahead = dot(inv, row[:, end : end + BLOCK], 1, 0)
        corner = rest[BLOCK : 2 * BLOCK, end : end + BLOCK] - dot(ahead, ahead, 0, 0)
        full = dot(inv, row, 1, 0)
        joined = jnp.concatenate(([full[:, :at]] if at else []) + [inv, full[:, end:]], 1)
        lane = lax.broadcasted_iota(jnp.int32, (BLOCK, n), 1)
        out[at:end, :] = jnp.where(lane < end, joined, 0.0)
        ready(at, end)
        below = rest[BLOCK:]
        lane = lax.broadcasted_iota(jnp.int32, below.shape, 1)
        rest = jnp.where((lane >= at) & (lane < end), 0.0, below) - dot(joined[:, end:], joined, 0, 0)


def sketch_kernel(total, few, test, test_other, standard, standard_other, tests, high, mid):
    samp, core = lax.axis_index("samp"), lax.axis_index("mark")
    side, count = test.shape[0], test.shape[0] // few
    for ref, at in ((test, 0), (test_other, side)):
        for i in range(count):
            row = pl.multiple_of(at + (samp ^ source(i, count)) * few, few)
            tests[pl.ds(row, few), :] = ref[i * few : (i + 1) * few, :]
    share = high.shape[0]
    rows = pl.ds(pl.multiple_of(core * share, share), share)
    sketch = dot(standard[rows, :], tests[:side, :], 1, 0, lax.Precision.DEFAULT) + dot(
        standard_other[rows, :], tests[side:, :], 1, 0, lax.Precision.DEFAULT
    )
    high[...], mid[...], _ = pieces(math.sqrt(total) * sketch)


def final_kernel(blocks, others, gathered, sketch_high, sketch_mid, basis, loadings, moments, inverse, product, *slots):
    samp, core = lax.axis_index("samp"), lax.axis_index("mark")
    side = 2 * HALF
    block = lambda ref, i: ref[i * HALF : (i + 1) * HALF, :]
    for ref, at in ((blocks, 0), (others, side)):
        corner = block(ref, 0)
        moments[at + HALF : at + side, at : at + HALF] = corner
        moments[at : at + HALF, at + HALF : at + side] = corner.T
        firsts = ref[3 * HALF + 2 * SQUARE :, :]
        for h in range(2):
            lower = ref[3 * HALF + h * SQUARE : 3 * HALF + (h + 1) * SQUARE, :]
            top, columns = at + h * HALF, slice(at + h * HALF, at + (h + 1) * HALF)
            moments[top : top + SQUARE, columns] = jnp.concatenate(
                [firsts[:, h * SQUARE : (h + 1) * SQUARE], lower[:, :SQUARE].T], 1
            )
            moments[top + SQUARE : top + HALF, columns] = lower
    mine, theirs = (block(blocks, 1), block(blocks, 2)), (block(others, 1), block(others, 2))
    for h in range(2):
        column = pl.ds(pl.multiple_of(side + (h + core - 2 * h * core) * HALF, HALF), HALF)
        moments[h * HALF : (h + 1) * HALF, column] = mine[h]
        moments[column, h * HALF : (h + 1) * HALF] = mine[h].T
        away = 1 - core
        column = pl.ds(pl.multiple_of((h + away - 2 * h * away) * HALF, HALF), HALF)
        moments[side + h * HALF : side + (h + 1) * HALF, column] = theirs[h]
        moments[column, side + h * HALF : side + (h + 1) * HALF] = theirs[h].T
    tests = gathered[...]
    product[...] = dot_pieces(pieces(moments[...]), tests, 1, 0)
    gram = dot_pieces_right(tests, pieces(product[...]), 0, 0)
    few = loadings.shape[0]
    own = product[pl.ds(pl.multiple_of(samp * few, few), few), :]

    def ready(at, end):
        high, mid, _ = pieces(inverse[at:end, :end])
        once = lambda a, b: dot(a[:, :end], b, 1, 1, lax.Precision.DEFAULT)
        basis[:, at:end] = once(sketch_high, high) + (once(sketch_high, mid) + once(sketch_mid, high))
        loadings[:, at:end] = dot(own[:, :end], inverse[at:end, :end], 1, 1)

    inverse_factor(gram, inverse, ready, *slots)


def call(kernel, shapes, inputs, scratch=()):
    vmem = pl.BlockSpec(memory_space=VMEM)
    many = isinstance(shapes, (list, tuple))
    return pl.pallas_call(
        kernel,
        out_shape=shapes,
        in_specs=[vmem] * len(inputs),
        out_specs=[vmem] * len(shapes) if many else vmem,
        scratch_shapes=list(scratch),
        compiler_params=pltpu.CompilerParams(vmem_limit_bytes=24 * 2**20),
    )(*inputs)


def swap(x, axis, bit):
    return lax.ppermute(x, axis, [(i, i ^ bit) for i in range(lax.axis_size(axis))])


def swap_by_core(x, bits):
    pairs = [(2 * i + c, 2 * (i ^ bits[c]) + c) for i in range(lax.axis_size("samp")) for c in range(2)]
    return lax.ppermute(x, ("samp", "mark"), pairs)


def upper(bits):
    mine = jnp.where(lax.axis_index("mark") == 0, bits[0], bits[1])
    return (lax.axis_index("samp") & mine) != 0


def in_order(x, got, up):
    return jnp.where(up, jnp.concatenate([got, x], 0), jnp.concatenate([x, got], 0))


def samp_bits():
    return [1 << i for i in range((lax.axis_size("samp") - 1).bit_length())]


def step_kernel(x, got, blocks, got_blocks, total, joined):
    total[...] = x[...] + got[...]
    joined[: blocks.shape[0], :] = blocks[...]
    joined[blocks.shape[0] :, :] = got_blocks[...]


def sum_plan(count):
    bits = [1 << i for i in range((count - 1).bit_length())]
    return list(zip(bits[:1] + bits[2:3] + bits[1:2] + bits[3:], bits))


def gather_plan(count):
    return [1 << i for i in reversed(range((count - 1).bit_length()))]


def source(i, count):
    return sum(bit for n, bit in enumerate(gather_plan(count)) if i >> n & 1)


def sum_and_gather(x, test, got_test):
    count = lax.axis_size("samp")
    sums, gathers = sum_plan(count), gather_plan(count)
    half, up = x.shape[0] // 2, upper(sums[0])
    kept = jnp.where(up, x[half:], x[:half])
    sent = jnp.where(up, x[:half], x[half:])
    test = jnp.concatenate([test, got_test], 0)
    for step, pair in enumerate(sums):
        got = swap_by_core(sent, pair)
        if step + 1 < len(gathers):
            got_test = swap(test, "samp", gathers[step + 1])
            kept, test = call(
                step_kernel,
                [
                    jax.ShapeDtypeStruct(kept.shape, kept.dtype),
                    jax.ShapeDtypeStruct((2 * test.shape[0], test.shape[1]), test.dtype),
                ],
                [kept, got, test, got_test],
            )
        else:
            kept = kept + got
        sent = kept
    test_other = swap(test, "mark", 1)
    got = swap_by_core(kept, sums[0])
    kept_other = swap(kept, "mark", 1)
    return in_order(kept, got, up), in_order(kept_other, swap(got, "mark", 1), up), test, test_other


def two_marks(dosage, alt_count, obs_count, sample_weight, test_matrix):
    rows, cols = dosage.shape
    few, rank = test_matrix.shape
    samples = rows * lax.axis_size("samp")
    standard = call(
        standard_kernel,
        jax.ShapeDtypeStruct((rows, cols), BF16),
        [dosage, alt_count.reshape(1, cols), obs_count.reshape(1, cols), sample_weight.reshape(1, rows)],
    )
    standard_other = swap(standard, "mark", 1)
    got_test = swap(test_matrix, "samp", gather_plan(lax.axis_size("samp"))[0])
    blocks = call(moment_kernel, jax.ShapeDtypeStruct((3 * HALF + 3 * SQUARE, HALF), F32), [standard, standard_other])
    blocks, others, test, test_other = sum_and_gather(blocks, test_matrix, got_test)
    prepare = lambda *refs: sketch_kernel(samples, few, *refs)
    share = jax.ShapeDtypeStruct((rows // 2, rank), BF16)
    prepared = call(
        prepare,
        [jax.ShapeDtypeStruct((2 * cols, rank), BF16), share, share],
        [test, test_other, standard, standard_other],
    )
    basis, loadings = call(
        final_kernel,
        [jax.ShapeDtypeStruct((rows // 2, rank), F32), jax.ShapeDtypeStruct((few, rank), F32)],
        [blocks, others, *prepared],
        [
            VMEM((2 * cols, 2 * cols), F32),
            VMEM((rank, rank), F32),
            VMEM((2 * cols, rank), F32),
            VMEM((36, 8, BLOCK), F32),
            VMEM((32, 8, BLOCK), F32),
        ],
    )
    return basis, loadings


def any_marks(dosage, alt_count, obs_count, sample_weight, test_matrix):
    freq = alt_count.astype(F32) / (2.0 * obs_count.astype(F32))
    scale = 1.0 / jnp.sqrt(2.0 * freq * (1.0 - freq))
    standard = (jnp.sqrt(sample_weight)[:, None] * (dosage.astype(F32) - 2.0 * freq) * scale).astype(BF16)
    rank = test_matrix.shape[1]
    partial_value = jnp.dot(
        standard, lax.all_gather(test_matrix, "samp", axis=0, tiled=True), preferred_element_type=F32
    )
    share = standard.shape[0] // lax.axis_size("mark")
    sketch = lax.psum(partial_value, "mark")
    own_rows = lax.dynamic_slice_in_dim(sketch, lax.axis_index("mark") * share, share, 0)
    gram = dot(sketch, sketch, 0, 0)
    lower = jnp.linalg.cholesky(lax.psum(gram, "samp"))
    inverse = lax.linalg.triangular_solve(lower, jnp.eye(rank, dtype=F32), left_side=True, lower=True)
    basis = math.sqrt(standard.shape[0] * lax.axis_size("samp")) * dot(own_rows, inverse, 1, 1)
    projected = lax.psum_scatter(
        dot(standard, sketch.astype(BF16), 0, 0, lax.Precision.DEFAULT), "samp", scatter_dimension=0, tiled=True
    )
    return basis, dot(projected, inverse, 1, 1)


def solution(mesh):
    samp, mark = mesh.shape["samp"], mesh.shape["mark"]

    def per_device(dosage, *rest):
        samples, width = dosage.shape
        few, rank = rest[-1].shape
        fits = mark == 2 and samp >= 4 and samp & (samp - 1) == 0 and width == 2 * HALF
        fits = fits and samples % (2 * HALF) == 0 and rank % BLOCK == 0 and few % 16 == 0
        return (two_marks if fits else any_marks)(dosage, *rest)

    return jax.shard_map(
        per_device,
        mesh=mesh,
        in_specs=(P("samp", "mark"), P("mark"), P("mark"), P("samp"), P(("mark", "samp"), None)),
        out_specs=(P(("samp", "mark"), None), P(("mark", "samp"), None)),
        check_vma=False,
    )
```

```python
import math

import jax
import jax.numpy as jnp
from jax import lax
from jax.experimental import pallas as pl
from jax.experimental.pallas import tpu as pltpu
from jax.sharding import PartitionSpec as P

F32, BF16 = jnp.float32, jnp.bfloat16
HALF = 128
SQUARE = HALF // 2
BLOCK = 128
VMEM = pltpu.VMEM


def dot(a, b, ca, cb, precision=lax.Precision.HIGHEST):
    return lax.dot_general(
        a, b, (((ca,), (cb,)), ((), ())), precision=precision, preferred_element_type=F32
    )


def pieces(x):
    high = x.astype(BF16)
    rest = x - high.astype(F32)
    mid = rest.astype(BF16)
    return high, mid, (rest - mid.astype(F32)).astype(BF16)


def dot_pieces(parts, b, ca, cb):
    terms = [dot(p, b, ca, cb, lax.Precision.DEFAULT) for p in parts]
    return terms[0] + (terms[1] + terms[2])


def dot_pieces_right(a, parts, ca, cb):
    terms = [dot(a, p, ca, cb, lax.Precision.DEFAULT) for p in parts]
    return terms[0] + (terms[1] + terms[2])


def standard_kernel(dosage, alt, obs, weight, out):
    freq = alt[...].astype(F32) / (2.0 * obs[...].astype(F32))
    scale = 1.0 / jnp.sqrt(2.0 * freq * (1.0 - freq))
    root = jnp.sqrt(weight[...])
    rows, cols = dosage.shape
    for r in range(0, rows, HALF):
        column = jnp.transpose(jnp.broadcast_to(root[:, r : r + HALF], (HALF, HALF)))
        for c in range(0, cols, HALF):
            x = dosage[r : r + HALF, c : c + HALF].astype(F32)
            f = freq[:, c : c + HALF]
            out[r : r + HALF, c : c + HALF] = (column * (x - 2.0 * f) * scale[:, c : c + HALF]).astype(BF16)


def moment_kernel(own, other, out):
    core = lax.axis_index("mark")
    low, high = own[:, :HALF], own[:, HALF:]
    first = other[:, pl.ds(pl.multiple_of(core * HALF, HALF), HALF)]
    second = other[:, pl.ds(pl.multiple_of((1 - core) * HALF, HALF), HALF)]
    for i, (a, b) in enumerate(((high, low), (low, first), (high, second))):
        out[i * HALF : (i + 1) * HALF, :] = dot(a, b, 0, 0, lax.Precision.DEFAULT)
    squares = [dot(a, a, 0, 0, lax.Precision.DEFAULT) for a in (low, high)]
    at = 3 * HALF
    for x in [x[SQUARE:] for x in squares] + [jnp.concatenate([x[:SQUARE, :SQUARE] for x in squares], 1)]:
        out[at : at + SQUARE, :] = x
        at += SQUARE


def eliminate(groups, slots, factor_slots):
    shape = groups[0].shape
    lane = lax.broadcasted_iota(jnp.int32, shape, 1)
    sub = lax.broadcasted_iota(jnp.int32, shape, 0)
    spread = lambda x: jnp.broadcast_to(x, shape)
    columns = lambda x, j: [jnp.take_along_axis(x, jnp.full(shape, j + k, jnp.int32), axis=1) for k in range(8)]
    groups, result = list(groups), []
    pivots = columns(groups[0], 0)
    for g in range(len(groups)):
        j, last = 8 * g, g + 1 == len(groups)
        slot, factor_slot = 9 * (g % 4), 8 * (g % 4)
        slots[slot + 8] = groups[g]
        rows = [spread(slots[slot + 8, k : k + 1, :]) for k in range(8)]
        for k in range(8):
            slots[slot + k] = pivots[k]
        a = {(i, k): spread(slots[slot + k, i : i + 1, :]) for k in range(8) for i in range(k, 8)}
        inside = (lane >= j) & (lane < j + 8)
        root, done, low, factors = [], [], {}, []
        block = jnp.zeros(shape, F32)
        if not last:
            left = columns(groups[g + 1], j)
            pivots = columns(groups[g + 1], j + 8)
            ahead = jnp.where(inside, 0.0, groups[g + 1])
        for k in range(8):
            q = lax.rsqrt(a[k, k])
            root.append(q)
            for i in range(k + 1, 8):
                low[i, k] = a[i, k] * q
            for i in range(k + 1, 8):
                for m in range(k + 1, i + 1):
                    a[i, m] = a[i, m] - low[i, k] * low[m, k]
            row = jnp.where(inside, jnp.where(lane == j + k, 1.0, 0.0), rows[k])
            for m in range(k):
                row = row - low[k, m] * done[m]
            done.append(row * q)
            block = jnp.where((sub == k) & (lane <= j + k), done[k], block)
            if not last:
                c = left[k]
                for m in range(k):
                    c = c - factors[m] * low[k, m]
                factors.append(c * q)
                factor_slots[factor_slot + k] = factors[k]
                for i in range(8):
                    pivots[i] = pivots[i] - factors[k] * spread(factor_slots[factor_slot + k, i : i + 1, :])
                ahead = ahead - factors[k] * done[k]
        result.append(block)
        if last:
            break
        groups[g + 1] = ahead
        update = [None] * 8
        for k in reversed(range(8)):
            x = done[k]
            for m in range(k + 1, 8):
                x = x - low[m, k] * update[m]
            update[k] = x * root[k]
        for n in range(g + 2, len(groups)):
            x = jnp.where(inside, 0.0, groups[n])
            for k, c in enumerate(columns(groups[n], j)):
                x = x - c * update[k]
            groups[n] = x
    return result


def inverse_factor(gram, out, ready, *slots):
    n = gram.shape[0]
    rest, corner = gram, gram[:BLOCK, :BLOCK]
    for at in range(0, n, BLOCK):
        end = at + BLOCK
        row = rest[:BLOCK]
        inv = jnp.concatenate(eliminate([corner[i : i + 8, :] for i in range(0, BLOCK, 8)], *slots), 0)
        if end == n:
            out[at:end, :] = jnp.concatenate([dot(inv, row[:, :at], 1, 0), inv], 1) if at else inv
            ready(at, end)
            break
        ahead = dot(inv, row[:, end : end + BLOCK], 1, 0)
        corner = rest[BLOCK : 2 * BLOCK, end : end + BLOCK] - dot(ahead, ahead, 0, 0)
        left = [dot(inv, row[:, :at], 1, 0)] if at else []
        right = [dot(inv, row[:, end + BLOCK :], 1, 0)] if end + BLOCK < n else []
        joined = jnp.concatenate(left + [inv, ahead] + right, 1)
        lane = lax.broadcasted_iota(jnp.int32, (BLOCK, n), 1)
        out[at:end, :] = jnp.where(lane < end, joined, 0.0)
        ready(at, end)
        stop = n if right else end
        below = rest[BLOCK:, :stop]
        lane = lax.broadcasted_iota(jnp.int32, below.shape, 1)
        rest = jnp.where((lane >= at) & (lane < end), 0.0, below) - dot(joined[:, end:], joined[:, :stop], 0, 0)


def sketch_kernel(total, few, test, test_other, standard, standard_other, tests, high, mid):
    samp, core = lax.axis_index("samp"), lax.axis_index("mark")
    side, count = test.shape[0], test.shape[0] // few
    for ref, at in ((test, 0), (test_other, side)):
        for i in range(count):
            row = pl.multiple_of(at + (samp ^ source(i, count)) * few, few)
            tests[pl.ds(row, few), :] = ref[i * few : (i + 1) * few, :]
    share = high.shape[0]
    rows = pl.ds(pl.multiple_of(core * share, share), share)
    sketch = dot(standard[rows, :], tests[:side, :], 1, 0, lax.Precision.DEFAULT) + dot(
        standard_other[rows, :], tests[side:, :], 1, 0, lax.Precision.DEFAULT
    )
    high[...], mid[...], _ = pieces(math.sqrt(total) * sketch)


def final_kernel(blocks, others, gathered, sketch_high, sketch_mid, basis, loadings, moments, inverse, product, *slots):
    samp, core = lax.axis_index("samp"), lax.axis_index("mark")
    side = 2 * HALF
    block = lambda ref, i: ref[i * HALF : (i + 1) * HALF, :]
    for ref, at in ((blocks, 0), (others, side)):
        corner = block(ref, 0)
        moments[at + HALF : at + side, at : at + HALF] = corner
        moments[at : at + HALF, at + HALF : at + side] = corner.T
        firsts = ref[3 * HALF + 2 * SQUARE :, :]
        for h in range(2):
            lower = ref[3 * HALF + h * SQUARE : 3 * HALF + (h + 1) * SQUARE, :]
            top, columns = at + h * HALF, slice(at + h * HALF, at + (h + 1) * HALF)
            moments[top : top + SQUARE, columns] = jnp.concatenate(
                [firsts[:, h * SQUARE : (h + 1) * SQUARE], lower[:, :SQUARE].T], 1
            )
            moments[top + SQUARE : top + HALF, columns] = lower
    mine, theirs = (block(blocks, 1), block(blocks, 2)), (block(others, 1), block(others, 2))
    for h in range(2):
        column = pl.ds(pl.multiple_of(side + (h + core - 2 * h * core) * HALF, HALF), HALF)
        moments[h * HALF : (h + 1) * HALF, column] = mine[h]
        moments[column, h * HALF : (h + 1) * HALF] = mine[h].T
        away = 1 - core
        column = pl.ds(pl.multiple_of((h + away - 2 * h * away) * HALF, HALF), HALF)
        moments[side + h * HALF : side + (h + 1) * HALF, column] = theirs[h]
        moments[column, side + h * HALF : side + (h + 1) * HALF] = theirs[h].T
    tests = gathered[...]
    product[...] = dot_pieces(pieces(moments[...]), tests, 1, 0)
    gram = dot_pieces_right(tests, pieces(product[...]), 0, 0)
    few = loadings.shape[0]
    own = product[pl.ds(pl.multiple_of(samp * few, few), few), :]

    def ready(at, end):
        high, mid, _ = pieces(inverse[at:end, :end])
        once = lambda a, b: dot(a[:, :end], b, 1, 1, lax.Precision.DEFAULT)
        basis[:, at:end] = once(sketch_high, high) + (once(sketch_high, mid) + once(sketch_mid, high))
        loadings[:, at:end] = dot(own[:, :end], inverse[at:end, :end], 1, 1)

    inverse_factor(gram, inverse, ready, *slots)


def call(kernel, shapes, inputs, scratch=()):
    vmem = pl.BlockSpec(memory_space=VMEM)
    many = isinstance(shapes, (list, tuple))
    return pl.pallas_call(
        kernel,
        out_shape=shapes,
        in_specs=[vmem] * len(inputs),
        out_specs=[vmem] * len(shapes) if many else vmem,
        scratch_shapes=list(scratch),
        compiler_params=pltpu.CompilerParams(vmem_limit_bytes=24 * 2**20),
    )(*inputs)


def swap(x, axis, bit):
    return lax.ppermute(x, axis, [(i, i ^ bit) for i in range(lax.axis_size(axis))])


def swap_by_core(x, bits):
    pairs = [(2 * i + c, 2 * (i ^ bits[c]) + c) for i in range(lax.axis_size("samp")) for c in range(2)]
    return lax.ppermute(x, ("samp", "mark"), pairs)


def upper(bits):
    mine = jnp.where(lax.axis_index("mark") == 0, bits[0], bits[1])
    return (lax.axis_index("samp") & mine) != 0


def in_order(x, got, up):
    return jnp.where(up, jnp.concatenate([got, x], 0), jnp.concatenate([x, got], 0))


def samp_bits():
    return [1 << i for i in range((lax.axis_size("samp") - 1).bit_length())]


def step_kernel(x, got, blocks, got_blocks, total, joined):
    total[...] = x[...] + got[...]
    joined[: blocks.shape[0], :] = blocks[...]
    joined[blocks.shape[0] :, :] = got_blocks[...]


def sum_plan(count):
    bits = [1 << i for i in range((count - 1).bit_length())]
    return list(zip(bits[:1] + bits[2:3] + bits[1:2] + bits[3:], bits))


def gather_plan(count):
    return [1 << i for i in reversed(range((count - 1).bit_length()))]


def source(i, count):
    return sum(bit for n, bit in enumerate(gather_plan(count)) if i >> n & 1)


def sum_and_gather(x, test, got_test):
    count = lax.axis_size("samp")
    sums, gathers = sum_plan(count), gather_plan(count)
    half, up = x.shape[0] // 2, upper(sums[0])
    kept = jnp.where(up, x[half:], x[:half])
    sent = jnp.where(up, x[:half], x[half:])
    test = jnp.concatenate([test, got_test], 0)
    for step, pair in enumerate(sums):
        got = swap_by_core(sent, pair)
        if step + 1 < len(gathers):
            got_test = swap(test, "samp", gathers[step + 1])
            kept, test = call(
                step_kernel,
                [
                    jax.ShapeDtypeStruct(kept.shape, kept.dtype),
                    jax.ShapeDtypeStruct((2 * test.shape[0], test.shape[1]), test.dtype),
                ],
                [kept, got, test, got_test],
            )
        else:
            kept = kept + got
        sent = kept
    test_other = swap(test, "mark", 1)
    got = swap_by_core(kept, sums[0])
    kept_other = swap(kept, "mark", 1)
    return in_order(kept, got, up), in_order(kept_other, swap(got, "mark", 1), up), test, test_other


def two_marks(dosage, alt_count, obs_count, sample_weight, test_matrix):
    rows, cols = dosage.shape
    few, rank = test_matrix.shape
    samples = rows * lax.axis_size("samp")
    standard = call(
        standard_kernel,
        jax.ShapeDtypeStruct((rows, cols), BF16),
        [dosage, alt_count.reshape(1, cols), obs_count.reshape(1, cols), sample_weight.reshape(1, rows)],
    )
    standard_other = swap(standard, "mark", 1)
    got_test = swap(test_matrix, "samp", gather_plan(lax.axis_size("samp"))[0])
    blocks = call(moment_kernel, jax.ShapeDtypeStruct((3 * HALF + 3 * SQUARE, HALF), F32), [standard, standard_other])
    blocks, others, test, test_other = sum_and_gather(blocks, test_matrix, got_test)
    prepare = lambda *refs: sketch_kernel(samples, few, *refs)
    share = jax.ShapeDtypeStruct((rows // 2, rank), BF16)
    prepared = call(
        prepare,
        [jax.ShapeDtypeStruct((2 * cols, rank), BF16), share, share],
        [test, test_other, standard, standard_other],
    )
    basis, loadings = call(
        final_kernel,
        [jax.ShapeDtypeStruct((rows // 2, rank), F32), jax.ShapeDtypeStruct((few, rank), F32)],
        [blocks, others, *prepared],
        [
            VMEM((2 * cols, 2 * cols), F32),
            VMEM((rank, rank), F32),
            VMEM((2 * cols, rank), F32),
            VMEM((36, 8, BLOCK), F32),
            VMEM((32, 8, BLOCK), F32),
        ],
    )
    return basis, loadings


def any_marks(dosage, alt_count, obs_count, sample_weight, test_matrix):
    freq = alt_count.astype(F32) / (2.0 * obs_count.astype(F32))
    scale = 1.0 / jnp.sqrt(2.0 * freq * (1.0 - freq))
    standard = (jnp.sqrt(sample_weight)[:, None] * (dosage.astype(F32) - 2.0 * freq) * scale).astype(BF16)
    rank = test_matrix.shape[1]
    partial_value = jnp.dot(
        standard, lax.all_gather(test_matrix, "samp", axis=0, tiled=True), preferred_element_type=F32
    )
    share = standard.shape[0] // lax.axis_size("mark")
    sketch = lax.psum(partial_value, "mark")
    own_rows = lax.dynamic_slice_in_dim(sketch, lax.axis_index("mark") * share, share, 0)
    gram = dot(sketch, sketch, 0, 0)
    lower = jnp.linalg.cholesky(lax.psum(gram, "samp"))
    inverse = lax.linalg.triangular_solve(lower, jnp.eye(rank, dtype=F32), left_side=True, lower=True)
    basis = math.sqrt(standard.shape[0] * lax.axis_size("samp")) * dot(own_rows, inverse, 1, 1)
    projected = lax.psum_scatter(
        dot(standard, sketch.astype(BF16), 0, 0, lax.Precision.DEFAULT), "samp", scatter_dimension=0, tiled=True
    )
    return basis, dot(projected, inverse, 1, 1)


def solution(mesh):
    samp, mark = mesh.shape["samp"], mesh.shape["mark"]

    def per_device(dosage, *rest):
        samples, width = dosage.shape
        few, rank = rest[-1].shape
        fits = mark == 2 and samp >= 4 and samp & (samp - 1) == 0 and width == 2 * HALF
        fits = fits and samples % (2 * HALF) == 0 and rank % BLOCK == 0 and few % 16 == 0
        return (two_marks if fits else any_marks)(dosage, *rest)

    return jax.shard_map(
        per_device,
        mesh=mesh,
        in_specs=(P("samp", "mark"), P("mark"), P("mark"), P("samp"), P(("mark", "samp"), None)),
        out_specs=(P(("samp", "mark"), None), P(("mark", "samp"), None)),
        check_vma=False,
    )
```
